128 devices in a mesh: gx: 8 (over y, x_lo), gy: 4 (over x_hi, core), gz: 4 (over z).
Axes of the slice: x: 4 (x_hi: 2, x_lo: 2; x = x_hi * 2 + x_lo), y: 4, z: 4, core: 2. Of those that a mesh axis runs over, the one named last changes fastest.
Arguments:
- latent: float32 [128, 64, 2048], P('gx', 'gy', 'gz'), may hold values from -6 to 6
- conv_first: bfloat16 [3, 3, 192, 64], replicated, may hold values from -0.15625 to 0.15625
- conv_second: bfloat16 [3, 3, 192, 64], replicated, may hold values from -0.15625 to 0.15625
- time_weight: float32 [64, 64], replicated, may hold values from -0.75 to 0.75
- timesteps: int32 [4], replicated, may hold values from 1 to 999
- offsets: int32 [4, 3], replicated, may hold values from 0 to 1, as said below
Outputs:
- denoised: float32 [128, 64, 2048], P('gx', 'gy', 'gz')
The draws below stay inside these ranges and needn't reach their ends.
Inputs may be any that keep to these rules, and one draw needn't show every extreme that they name: `offsets`: every entry is 0 or 1, and each of the three columns holds at least one 0 and at least one 1.
All inputs are finite; a program needn't handle non-finite values.
Results may differ from the reference program's by a relative error of at most 0.0055.
Values sent between devices are 32-bit elements; how exact they have to be, the bound alone decides.
A program may use at most 64 MiB of HBM per device.

```python
import math
import jax
import jax.numpy as jnp
from jax import lax

C = 64
CX = 16
CY = 16
CZ = 8
STEPS = 4
NX = 128
NY = 64
NZ = 32
N_GX = 8
N_GY = 4
N_GZ = 4


def draw_offsets(key, part):
    columns = []
    for axis_number in range(3):
        subkey = jax.random.fold_in(key, 17 + axis_number)
        first_key, second_key = jax.random.split(subkey)
        extra = jax.random.randint(first_key, (STEPS - 2,), 0, 2).astype(jnp.int32)
        base = jnp.concatenate([jnp.array([0, 1], dtype=jnp.int32), extra])
        columns.append(jax.random.permutation(second_key, base))
    return jnp.stack(columns, axis=1).astype(jnp.int32)


def set_ends(result, key, least, high):
    longest = result.shape.index(max(result.shape))
    spots = []
    for shift in (0, 1):
        where = [jax.random.randint(jax.random.fold_in(key, axis), (), 0, length) for axis, length in enumerate(result.shape)]
        where[longest] = (where[longest] + shift) % result.shape[longest]
        spots.append(tuple(where))
    return result.at[spots[0]].set(least).at[spots[1]].set(high)


def block_scale(stream_key, dims, shards, least, top_value):
    def one(axis_at, blocks):
        draws = jax.random.uniform(jax.random.fold_in(jax.random.fold_in(stream_key, 6), axis_at), (blocks,), jnp.float32, least / len(shards), top_value / len(shards))
        return jnp.repeat(jnp.exp(draws), dims[axis_at] // blocks).reshape((-1,) + (1,) * (len(dims) - axis_at - 1))

    level = one(*shards[0])
    for cut in shards[1:]:
        level = level * one(*cut)
    return level


def gaussian(stream_key, shape, spread, bound, cuts=(), kind=jnp.bfloat16):
    values = spread * jax.random.normal(stream_key, shape, jnp.float32)
    if cuts:
        values = values * block_scale(stream_key, shape, cuts, -0.22, 0.18)
    return jnp.clip(values, -bound, bound).astype(kind)


def setup_inputs(seed: int = 0) -> dict:
    arg_keys = jax.random.split(jax.random.key(seed), 7)
    latent = gaussian(arg_keys[0], (NX, NY, NZ * C), 1.0, 6.0, ((0, 8), (1, 4), (2, 4)), jnp.float32)
    conv_first = gaussian(arg_keys[1], (3, 3, 3 * C, C), (27 * C) ** -0.5, 0.15625)
    conv_second = gaussian(arg_keys[2], (3, 3, 3 * C, C), (27 * C) ** -0.5, 0.15625)
    time_weight = gaussian(arg_keys[3], (C, C), C ** -0.5, 0.75, (), jnp.float32)
    timesteps = set_ends(jax.random.randint(arg_keys[4], (STEPS,), 1, 1000), jax.random.fold_in(arg_keys[4], 1), 1, 999).astype(jnp.int32)
    offsets = draw_offsets(jax.random.fold_in(arg_keys[6], 71), 0)
    return {"latent": latent, "conv_first": conv_first, "conv_second": conv_second, "time_weight": time_weight, "timesteps": timesteps, "offsets": offsets}


def time_bias(step_time, time_weight):
    half_c = C // 2
    freqs = jnp.exp(-math.log(10000.0) * jnp.arange(half_c, dtype=jnp.float32) / half_c)
    angles = step_time.astype(jnp.float32) * freqs
    emb = jnp.concatenate([jnp.sin(angles), jnp.cos(angles)])
    return jnp.dot(emb, time_weight, precision=lax.Precision.HIGHEST)


def to_windows(grid):
    parts = grid.reshape(N_GX, CX, N_GY, CY, N_GZ, CZ, C)
    parts = parts.transpose(0, 2, 4, 1, 3, 5, 6)
    return parts.reshape(N_GX * N_GY * N_GZ, CX, CY, CZ, C)


def from_windows(windows):
    parts = windows.reshape(N_GX, N_GY, N_GZ, CX, CY, CZ, C)
    parts = parts.transpose(0, 3, 1, 4, 2, 5, 6)
    return parts.reshape(NX, NY, NZ, C)


def window_conv(values, weight):
    kernel = weight.astype(jnp.float32).reshape(3, 3, 3, C, C)
    return lax.conv_general_dilated(values, kernel, (1, 1, 1), "SAME", dimension_numbers=("NDHWC", "DHWIO", "NDHWC"), precision=lax.Precision.HIGHEST)


def reference(latent, conv_first, conv_second, time_weight, timesteps, offsets):
    grid = latent.reshape(NX, NY, NZ, C)
    for step in range(STEPS):
        move_x = offsets[step, 0] * (CX // 2)
        move_y = offsets[step, 1] * (CY // 2)
        move_z = offsets[step, 2] * (CZ // 2)
        shifted = jnp.roll(grid, -move_x, axis=0)
        shifted = jnp.roll(shifted, -move_y, axis=1)
        shifted = jnp.roll(shifted, -move_z, axis=2)
        windows = to_windows(shifted)
        inputs = lax.optimization_barrier(windows.astype(jnp.bfloat16)).astype(jnp.float32)
        bias = time_bias(timesteps[step], time_weight)
        hidden = jax.nn.silu(window_conv(inputs, conv_first) + bias)
        hidden = lax.optimization_barrier(hidden.astype(jnp.bfloat16)).astype(jnp.float32)
        noise = window_conv(hidden, conv_second)
        if step + 1 < STEPS:
            next_time = timesteps[step + 1]
        else:
            next_time = jnp.zeros((), jnp.int32)
        delta = (next_time - timesteps[step]).astype(jnp.float32) / 1000.0
        updated = from_windows(windows + delta * noise)
        updated = jnp.roll(updated, move_z, axis=2)
        updated = jnp.roll(updated, move_y, axis=1)
        grid = jnp.roll(updated, move_x, axis=0)
    return grid.reshape(NX, NY, NZ * C)
```

```python
import itertools
import math

import jax
import jax.numpy as jnp
from jax import lax
from jax.experimental import pallas as pl
from jax.experimental.pallas import tpu as pltpu
from jax.sharding import PartitionSpec as P

MESH = pl.DeviceIdType.MESH
F32 = jnp.float32
BF16 = jnp.bfloat16

XS, YS, TILES = 26, 24, 6


def directions():
    every = [d for d in itertools.product((-1, 0, 1), repeat=3) if d != (0, 0, 0)]
    return sorted(every, key=lambda d: -sum(map(abs, d)))


DIRECTIONS = directions()


def sent(d):
    x = {-1: pl.ds(2, 2), 0: pl.ds(2, 16), 1: pl.ds(16, 2)}[d[0]]
    y = {-1: pl.ds(0, 2), 0: pl.ds(0, 16), 1: pl.ds(14, 2)}[d[1]]
    z = {-1: pl.ds(0, 1), 0: pl.ds(0, 4), 1: pl.ds(3, 1)}[d[2]]
    return z, x, y


def landed(d):
    x = {-1: pl.ds(18, 2), 0: pl.ds(2, 16), 1: pl.ds(0, 2)}[d[0]]
    y = {-1: pl.ds(16, 2), 0: pl.ds(0, 16), 1: pl.ds(22, 2)}[d[1]]
    z = {-1: pl.ds(4, 1), 0: pl.ds(0, 4), 1: pl.ds(5, 1)}[d[2]]
    return z, x, y


def neighbour(d):
    place = []
    for name, by in zip(("gx", "gy", "gz"), d):
        size = lax.axis_size(name)
        place.append(lax.rem(lax.axis_index(name) + by + size, size))
    return tuple(place)


def kernel(
    steps, latent_ref, first_ref, second_ref, bias_ref, delta_ref, offsets_ref, out_ref,
    ext, w1, w1c, w2, taps_in, edge_in, hidden, taps_hid, send_sem, recv_sem, load_sem,
):
    loads = [
        pltpu.make_async_copy(
            latent_ref.at[:, :, pl.ds(128 * tile, 128)],
            ext.at[0, tile, pl.ds(2, 16), pl.ds(0, 16)],
            load_sem.at[tile],
        )
        for tile in range(4)
    ]
    for load in loads:
        load.start()
    barrier = pltpu.get_barrier_semaphore()
    for d in DIRECTIONS:
        pl.semaphore_signal(barrier, inc=1, device_id=neighbour(d), device_id_type=MESH)
    pl.semaphore_wait(barrier, len(DIRECTIONS))
    for load in loads:
        load.wait()

    def copies(step):
        return [
            pltpu.make_async_remote_copy(
                src_ref=ext.at[(step, *sent(d))],
                dst_ref=ext.at[(step, *landed(d))],
                send_sem=send_sem.at[step, i],
                recv_sem=recv_sem.at[step, i],
                device_id=neighbour(d),
                device_id_type=MESH,
            )
            for i, d in enumerate(DIRECTIONS)
        ]

    for copy in copies(0):
        copy.start()

    w1[...] = jnp.zeros_like(w1)
    w1c[...] = jnp.zeros_like(w1c)
    w2[...] = jnp.zeros_like(w2)

    def place_weights(tap, carry):
        one = first_ref[tap]
        two = second_ref[tap]
        for out in range(4):
            rows = pl.ds(out * 64, 192)
            lanes = pl.ds(out * 64, 64)
            w1[0, tap, rows, lanes] = one
            w2[tap, rows, lanes] = two
            if out < 2:
                w1c[tap, rows, lanes] = one
        w1[1, tap, pl.ds(0, 128), pl.ds(0, 64)] = one[:128]
        w1[1, tap, pl.ds(128, 128), pl.ds(64, 64)] = one[64:]
        w1[1, tap, pl.ds(128, 192), pl.ds(128, 64)] = one
        w1[1, tap, pl.ds(192, 192), pl.ds(192, 64)] = one
        return carry

    lax.fori_loop(0, 9, place_weights, 0)

    row16 = lax.broadcasted_iota(jnp.int32, (16, 128), 0)

    def step_body(step, carry):
        for copy in copies(step):
            copy.wait_recv()

        flag_x = offsets_ref[step, 0]
        flag_y = offsets_ref[step, 1]
        flag_z = offsets_ref[step, 2]
        on_x = flag_x.astype(F32)
        on_z = flag_z.astype(F32)
        off_x = 1.0 - on_x
        cut_down = row16 == 8 * flag_y
        cut_up = row16 == 15 - 8 * flag_y

        def three_rows(value):
            down = pltpu.roll(value, 1, 0)[:16]
            up = pltpu.roll(value, YS - 1, 0)[:16]
            return jnp.where(cut_down, 0.0, down), value[:16], jnp.where(cut_up, 0.0, up)

        def input_slot(slot, carry):
            outside = jnp.logical_or(slot < 2, slot >= 18)
            keep = jnp.where(outside, on_x, 1.0)
            to = slot + 2 * (slot >= 10).astype(jnp.int32)
            for tile in range(TILES):
                value = ext[step, tile, slot] * (keep if tile < 4 else keep * on_z)
                for tap, rows in enumerate(three_rows(value)):
                    taps_in[tap, to, :, pl.ds(128 * tile, 128)] = rows.astype(BF16)
            return carry

        lax.fori_loop(0, 20, input_slot, 0)
        for tap in range(3):
            taps_in[tap, 10] = (taps_in[tap, 12].astype(F32) * off_x).astype(BF16)
            taps_in[tap, 11] = (taps_in[tap, 9].astype(F32) * off_x).astype(BF16)

        flat = ext.at[step].reshape(TILES, XS * YS, 128)
        slot24 = lax.broadcasted_iota(jnp.int32, (24, 128), 0)
        for tap_x in range(3):
            entry = slot24 + tap_x
            outside = jnp.logical_or(entry < 2, entry >= 18)
            keep = jnp.where(outside, on_x, 1.0)
            if tap_x == 0:
                keep = jnp.where(slot24 == 9, off_x, keep)
            if tap_x == 2:
                keep = jnp.where(slot24 == 8, off_x, keep)
            keep_halo = keep * on_z
            for tap_y in range(3):
                for tile in range(TILES):
                    parts = []
                    for row in ((22 + tap_y) % 24, 15 + tap_y):
                        value = flat[tile, pl.ds(tap_x * YS + row, 24, stride=YS), :]
                        parts.append(value * (keep if tile < 4 else keep_halo))
                    place = pl.ds(128 * tile, 128)
                    edge_in[3 * tap_x + tap_y, :, place] = jnp.concatenate(parts, axis=0).astype(BF16)

        def inputs_for(tiles):
            columns = []
            for tap_x in range(3):
                for tap_y in range(3):
                    for tile in tiles:
                        lanes = pl.ds(tile * 128, 128)
                        columns.append(jnp.concatenate([
                            taps_in[tap_y, pl.ds(tap_x, 9), :, lanes].reshape(144, 128),
                            taps_in[tap_y, pl.ds(11 + tap_x, 9), :, lanes].reshape(144, 128),
                            edge_in[3 * tap_x + tap_y, :, lanes],
                        ], axis=0))
            return jnp.concatenate(columns, axis=1)

        bias = bias_ref[step]
        flat_hidden = hidden.reshape(5, 24 * YS, 128)
        edge_keep = jnp.where(jnp.logical_or(slot24 < 1, slot24 >= 17), on_x, 1.0)

        def keep_hidden(total, tile, keep_lane):
            value = total + bias
            value = value / (1.0 + jnp.exp(-value))
            if keep_lane is not None:
                value = value * keep_lane
            for slot in range(18):
                part = value[16 * slot : 16 * slot + 16]
                if slot in (0, 17):
                    part = part * on_x
                hidden[tile, slot, pl.ds(0, 16)] = part
            for i, row in enumerate((23, 16)):
                part = value[288 + 24 * i : 312 + 24 * i] * edge_keep
                flat_hidden[tile, pl.ds(row, 24, stride=YS), :] = part

        lane128 = lax.broadcasted_iota(jnp.int32, (1, 128), 1)
        total = jnp.dot(inputs_for((5, 0, 1)), w1[0].reshape(3456, 256), preferred_element_type=F32)
        keep_hidden(total[:, :128], 0, jnp.where(lane128 < 64, on_z, 1.0))
        keep_hidden(total[:, 128:], 1, None)
        total = jnp.dot(inputs_for((1, 2, 3)), w1[flag_z].reshape(3456, 256), preferred_element_type=F32)
        keep_hidden(total[:, :128], 2, None)
        keep_hidden(total[:, 128:], 3, None)
        total = jnp.dot(inputs_for((3, 4)), w1c[...].reshape(2304, 128), preferred_element_type=F32)
        keep_hidden(total, 4, jnp.where(lane128 >= 64, on_z, 1.0))

        low = jnp.where(lane128 < 64, 1.0, 1.0 - on_z)
        high = jnp.where(lane128 >= 64, 1.0, 1.0 - on_z)

        def hidden_slot(slot, carry):
            to = slot + 2 * (slot >= 9).astype(jnp.int32)
            for place, (tile, keep) in enumerate(((0, None), (1, None), (2, low), (2, high), (3, None), (4, None))):
                value = hidden[tile, slot]
                if keep is not None:
                    value = value * keep
                for tap, rows in enumerate(three_rows(value)):
                    taps_hid[tap, to, :, pl.ds(128 * place, 128)] = rows.astype(BF16)
            return carry

        lax.fori_loop(0, 18, hidden_slot, 0)
        for tap in range(3):
            taps_hid[tap, 9] = (taps_hid[tap, 11].astype(F32) * off_x).astype(BF16)
            taps_hid[tap, 10] = (taps_hid[tap, 8].astype(F32) * off_x).astype(BF16)

        def hidden_for(tiles):
            columns = []
            for tap_x in range(3):
                for tap_y in range(3):
                    lanes = pl.ds(tiles * 128, 384)
                    columns.append(jnp.concatenate([
                        taps_hid[tap_y, pl.ds(tap_x, 8), :, lanes].reshape(128, 384),
                        taps_hid[tap_y, pl.ds(10 + tap_x, 8), :, lanes].reshape(128, 384),
                    ], axis=0))
            return jnp.concatenate(columns, axis=1)

        delta = delta_ref[step]
        for half in range(2):
            noise = jnp.dot(hidden_for(3 * half), w2[...].reshape(3456, 256), preferred_element_type=F32)
            for tile in range(2):
                part = noise[:, 128 * tile : 128 * tile + 128].reshape(16, 16, 128)
                before = ext[step, 2 * half + tile, pl.ds(2, 16), pl.ds(0, 16)]
                ext[step + 1, 2 * half + tile, pl.ds(2, 16), pl.ds(0, 16)] = before + delta * part

        @pl.when(step + 1 < steps)
        def _():
            for copy in copies(step + 1):
                copy.start()

        return carry

    lax.fori_loop(0, steps, step_body, 0)

    stores = [
        pltpu.make_async_copy(
            ext.at[steps, tile, pl.ds(2, 16), pl.ds(0, 16)],
            out_ref.at[:, :, pl.ds(128 * tile, 128)],
            load_sem.at[tile],
        )
        for tile in range(4)
    ]
    for store in stores:
        store.start()

    def drain(step, carry):
        for copy in copies(step):
            copy.wait_send()
        return carry

    lax.fori_loop(0, steps, drain, 0)
    for store in stores:
        store.wait()


def time_bias(timesteps, time_weight):
    half_c = time_weight.shape[0] // 2
    freqs = jnp.exp(-math.log(10000.0) * jnp.arange(half_c, dtype=F32) / half_c)
    angles = timesteps.astype(F32)[:, None] * freqs
    emb = jnp.concatenate([jnp.sin(angles), jnp.cos(angles)], axis=1)
    return jnp.dot(emb, time_weight, precision=lax.Precision.HIGHEST)


def shards(latent, conv_first, conv_second, time_weight, timesteps, offsets):
    steps = timesteps.shape[0]
    bias = time_bias(timesteps, time_weight)
    bias = jnp.concatenate([bias, bias], axis=1).reshape(steps, 1, 128)
    later = jnp.concatenate([timesteps[1:], jnp.zeros((1,), jnp.int32)])
    delta = (later - timesteps).astype(F32) / 1000.0
    vmem = pl.BlockSpec(memory_space=pltpu.VMEM)
    smem = pl.BlockSpec(memory_space=pltpu.SMEM)
    anywhere = pl.BlockSpec(memory_space=pl.ANY)
    count = len(DIRECTIONS)

    def body(*refs):
        kernel(steps, *refs)

    return pl.pallas_call(
        body,
        out_shape=jax.ShapeDtypeStruct(latent.shape, latent.dtype),
        in_specs=[anywhere, vmem, vmem, vmem, smem, smem],
        out_specs=anywhere,
        scratch_shapes=[
            pltpu.VMEM((steps + 1, TILES, XS, YS, 128), F32),
            pltpu.VMEM((2, 9, 384, 256), BF16),
            pltpu.VMEM((9, 256, 128), BF16),
            pltpu.VMEM((9, 384, 256), BF16),
            pltpu.VMEM((3, 22, 16, 768), BF16),
            pltpu.VMEM((9, 48, 768), BF16),
            pltpu.VMEM((5, 24, YS, 128), F32),
            pltpu.VMEM((3, 20, 16, 768), BF16),
            pltpu.SemaphoreType.DMA((steps, count)),
            pltpu.SemaphoreType.DMA((steps, count)),
            pltpu.SemaphoreType.DMA((4,)),
        ],
        compiler_params=pltpu.CompilerParams(
            collective_id=0, has_side_effects=True, vmem_limit_bytes=48 * 2**20
        ),
    )(latent, conv_first.reshape(9, 192, 64), conv_second.reshape(9, 192, 64), bias, delta, offsets)


def solution(mesh):
    return jax.shard_map(
        shards,
        mesh=mesh,
        in_specs=(P("gx", "gy", "gz"), P(), P(), P(), P(), P()),
        out_specs=P("gx", "gy", "gz"),
        check_vma=False,
    )
```

```python
import itertools
import math

import jax
import jax.numpy as jnp
from jax import lax
from jax.experimental import pallas as pl
from jax.experimental.pallas import tpu as pltpu
from jax.sharding import PartitionSpec as P

MESH = pl.DeviceIdType.MESH
F32 = jnp.float32
BF16 = jnp.bfloat16

XS, YS, TILES = 20, 24, 6


def directions():
    every = [d for d in itertools.product((-1, 0, 1), repeat=3) if d != (0, 0, 0)]
    return sorted(every, key=lambda d: (d[0] != 0, -sum(map(abs, d))))


DIRECTIONS = directions()


def sent(d):
    x = {-1: pl.ds(2, 2), 0: pl.ds(2, 16), 1: pl.ds(16, 2)}[d[0]]
    y = {-1: pl.ds(0, 2), 0: pl.ds(0, 16), 1: pl.ds(14, 2)}[d[1]]
    z = {-1: pl.ds(0, 1), 0: pl.ds(0, 4), 1: pl.ds(3, 1)}[d[2]]
    return z, x, y


def landed(d):
    x = {-1: pl.ds(18, 2), 0: pl.ds(2, 16), 1: pl.ds(0, 2)}[d[0]]
    y = {-1: pl.ds(16, 2), 0: pl.ds(0, 16), 1: pl.ds(22, 2)}[d[1]]
    z = {-1: pl.ds(4, 1), 0: pl.ds(0, 4), 1: pl.ds(5, 1)}[d[2]]
    return z, x, y


def neighbour(d):
    place = []
    for name, by in zip(("gx", "gy", "gz"), d):
        size = lax.axis_size(name)
        place.append(lax.rem(lax.axis_index(name) + by + size, size))
    return tuple(place)


def kernel(
    steps, latent_ref, first_ref, second_ref, bias_ref, delta_ref, offsets_ref, out_ref,
    ext, w1, w1c, w2, taps_in, edge_in, taps_side, edge_side, partial, hidden, taps_hid, send_sem, recv_sem, load_sem,
):
    loads = [
        pltpu.make_async_copy(
            latent_ref.at[:, :, pl.ds(128 * tile, 128)],
            ext.at[0, tile, pl.ds(2, 16), pl.ds(0, 16)],
            load_sem.at[tile],
        )
        for tile in range(4)
    ]
    for load in loads:
        load.start()
    barrier = pltpu.get_barrier_semaphore()
    for d in DIRECTIONS:
        pl.semaphore_signal(barrier, inc=1, device_id=neighbour(d), device_id_type=MESH)
    pl.semaphore_wait(barrier, len(DIRECTIONS))
    for load in loads:
        load.wait()

    def copies(step, sides=(-1, 0, 1)):
        return [
            pltpu.make_async_remote_copy(
                src_ref=ext.at[(step, *sent(d))],
                dst_ref=ext.at[(step, *landed(d))],
                send_sem=send_sem.at[step, i],
                recv_sem=recv_sem.at[step, i],
                device_id=neighbour(d),
                device_id_type=MESH,
            )
            for i, d in enumerate(DIRECTIONS)
            if d[0] in sides
        ]

    for copy in copies(0):
        copy.start()

    w1[...] = jnp.zeros_like(w1)
    w1c[...] = jnp.zeros_like(w1c)
    w2[...] = jnp.zeros_like(w2)

    def place_weights(tap, carry):
        one = first_ref[tap]
        two = second_ref[tap]
        for out in range(4):
            rows = pl.ds(out * 64, 192)
            lanes = pl.ds(out * 64, 64)
            w1[0, tap, rows, lanes] = one
            w2[tap, rows, lanes] = two
            if out < 2:
                w1c[tap, rows, lanes] = one
        w1[1, tap, pl.ds(0, 128), pl.ds(0, 64)] = one[:128]
        w1[1, tap, pl.ds(128, 128), pl.ds(64, 64)] = one[64:]
        w1[1, tap, pl.ds(128, 192), pl.ds(128, 64)] = one
        w1[1, tap, pl.ds(192, 192), pl.ds(192, 64)] = one
        return carry

    lax.fori_loop(0, 9, place_weights, 0)

    row8 = lax.broadcasted_iota(jnp.int32, (8, 128), 0)
    row16 = lax.broadcasted_iota(jnp.int32, (16, 128), 0)
    lane128 = lax.broadcasted_iota(jnp.int32, (1, 128), 1)
    own_rows = pl.ds(0, 16)

    def step_body(step, carry):
        flag_x = offsets_ref[step, 0]
        flag_y = offsets_ref[step, 1]
        flag_z = offsets_ref[step, 2]
        on_x = flag_x.astype(F32)
        on_y = flag_y.astype(F32)
        on_z = flag_z.astype(F32)
        off_x = 1.0 - on_x
        cut_down = row16 == 8 * flag_y
        cut_up = row16 == 15 - 8 * flag_y
        cut_back = jnp.logical_and(row16 == 8, flag_x == 1)
        cut_ahead = jnp.logical_and(row16 == 7, flag_x == 1)
        bias = bias_ref[step]
        delta = delta_ref[step]
        flat = ext.at[step].reshape(TILES, XS * YS, 128)
        flat_hidden = hidden.reshape(5, 18 * YS, 128)

        def three_rows(value):
            count = value.shape[0]
            down = pltpu.roll(value, 1, 0)[:16]
            up = pltpu.roll(value, count - 1, 0)[:16]
            return jnp.where(cut_down, 0.0, down), value[:16], jnp.where(cut_up, 0.0, up)

        def lanes_of(tile):
            return pl.ds(128 * tile, 128)

        def close_gap(taps, gap, tiles):
            lanes = pl.ds(128 * tiles[0], 128 * len(tiles))
            for tap in range(3):
                taps[tap, gap, :, lanes] = (taps[tap, gap + 2, :, lanes].astype(F32) * off_x).astype(BF16)
                taps[tap, gap + 1, :, lanes] = (taps[tap, gap - 1, :, lanes].astype(F32) * off_x).astype(BF16)

        def input_slots(tiles, keep):
            def one(x, carry):
                to = x + 2 * (x >= 8).astype(jnp.int32)
                for tile in tiles:
                    value = ext[step, tile, x + 2, own_rows]
                    if keep is not None:
                        value = value * keep
                    for tap, rows in enumerate(three_rows(value)):
                        taps_in[tap, to, :, lanes_of(tile)] = rows.astype(BF16)
                return carry

            lax.fori_loop(0, 16, one, 0)
            close_gap(taps_in, 8, tiles)

        def inner_inputs(tiles):
            columns = []
            for tap_x in range(3):
                for tap_y in range(3):
                    for tile in tiles:
                        columns.append(jnp.concatenate([
                            taps_in[tap_y, pl.ds(tap_x, 7), :, lanes_of(tile)].reshape(112, 128),
                            taps_in[tap_y, pl.ds(9 + tap_x, 7), :, lanes_of(tile)].reshape(112, 128),
                        ], axis=0))
            return jnp.concatenate(columns, axis=1)

        def silu(total, tile):
            value = total + bias
            value = value / (1.0 + jnp.exp(-value))
            if tile == 0:
                value = value * jnp.where(lane128 < 64, on_z, 1.0)
            if tile == 4:
                value = value * jnp.where(lane128 >= 64, on_z, 1.0)
            return value

        input_slots((0, 1, 2, 3), None)
        total = jnp.dot(
            inner_inputs((0, 1)), w1[0, :, pl.ds(128, 256), :].reshape(2304, 256), preferred_element_type=F32
        )
        partial[0] = total[:, :128]
        partial[1] = total[:, 128:]
        total = jnp.dot(inner_inputs((1, 2, 3)), w1[flag_z].reshape(3456, 256), preferred_element_type=F32)
        partial[2] = total[:, :128]
        partial[3] = total[:, 128:]
        partial[4] = jnp.dot(
            inner_inputs((3,)), w1c[:, pl.ds(0, 128), :].reshape(1152, 128), preferred_element_type=F32
        )

        for copy in copies(step, (0,)):
            copy.wait_recv()
        input_slots((4, 5), on_z)

        for place, row in enumerate((22, 23, 0, 1, 14, 15, 16, 17)):
            keep_row = on_y if row >= 16 else None
            for tile in range(TILES):
                value = flat[tile, pl.ds(2 * YS + row, 16, stride=YS), :]
                if keep_row is not None:
                    value = value * keep_row
                if tile >= 4:
                    value = value * on_z
                back = jnp.where(cut_back, 0.0, pltpu.roll(value, 1, 0))
                ahead = jnp.where(cut_ahead, 0.0, pltpu.roll(value, 15, 0))
                for tap, rows in enumerate((back, value, ahead)):
                    edge_in[tap, place, :, lanes_of(tile)] = rows.astype(BF16)

        def edge_inputs(tiles):
            columns = []
            for tap_x in range(3):
                for tap_y in range(3):
                    for tile in tiles:
                        columns.append(jnp.concatenate([
                            edge_in[tap_x, pl.ds(tap_y, 2), :, lanes_of(tile)].reshape(32, 128),
                            edge_in[tap_x, pl.ds(4 + tap_y, 2), :, lanes_of(tile)].reshape(32, 128),
                        ], axis=0))
            return jnp.concatenate(columns, axis=1)

        def keep_inner(total, tile):
            value = silu(total, tile)
            for x in range(1, 15):
                hidden[tile, x + 1, own_rows] = value[16 * x - 16 : 16 * x]

        def keep_edges(total, tile):
            value = silu(total, tile)
            for i, row in enumerate((23, 0, 15, 16)):
                flat_hidden[tile, pl.ds(YS + row, 16, stride=YS), :] = value[16 * i : 16 * i + 16]

        total = jnp.dot(
            inner_inputs((5,)), w1[0, :, pl.ds(0, 128), :].reshape(1152, 256), preferred_element_type=F32
        )
        keep_inner(partial[0] + total[:, :128], 0)
        keep_inner(partial[1] + total[:, 128:], 1)
        keep_inner(partial[2], 2)
        keep_inner(partial[3], 3)
        total = jnp.dot(
            inner_inputs((4,)), w1c[:, pl.ds(128, 128), :].reshape(1152, 128), preferred_element_type=F32
        )
        keep_inner(partial[4] + total, 4)
        total = jnp.dot(edge_inputs((5, 0, 1)), w1[0].reshape(3456, 256), preferred_element_type=F32)
        keep_edges(total[:, :128], 0)
        keep_edges(total[:, 128:], 1)
        total = jnp.dot(edge_inputs((1, 2, 3)), w1[flag_z].reshape(3456, 256), preferred_element_type=F32)
        keep_edges(total[:, :128], 2)
        keep_edges(total[:, 128:], 3)
        total = jnp.dot(edge_inputs((3, 4)), w1c[...].reshape(2304, 128), preferred_element_type=F32)
        keep_edges(total, 4)

        low = jnp.where(lane128 < 64, 1.0, 1.0 - on_z)
        high = jnp.where(lane128 >= 64, 1.0, 1.0 - on_z)

        def hidden_slot(slot, to, keep_x):
            sources = ((0, None), (1, None), (2, low), (2, high), (3, None), (4, None))
            for place, (tile, keep) in enumerate(sources):
                value = hidden[tile, slot]
                if keep is not None:
                    value = value * keep
                if keep_x is not None:
                    value = value * keep_x
                for tap, rows in enumerate(three_rows(value)):
                    taps_hid[tap, to, :, lanes_of(place)] = rows.astype(BF16)

        def inner_slot(slot, carry):
            hidden_slot(slot, slot + 2 * (slot >= 9).astype(jnp.int32), None)
            return carry

        lax.fori_loop(2, 16, inner_slot, 0)
        close_gap(taps_hid, 9, tuple(range(6)))

        def noise_of(half, low_slot, high_slot, slots):
            lanes = pl.ds(384 * half, 384)
            columns = []
            for tap_x in range(3):
                for tap_y in range(3):
                    columns.append(jnp.concatenate([
                        taps_hid[tap_y, pl.ds(start + tap_x, slots), :, lanes].reshape(16 * slots, 384)
                        for start in (low_slot, high_slot)
                    ], axis=0))
            values = jnp.concatenate(columns, axis=1)
            return jnp.dot(values, w2[...].reshape(3456, 256), preferred_element_type=F32)

        def update(noise, half, starts, slots):
            for part in range(2):
                tile = 2 * half + part
                for i, x in enumerate(starts):
                    place = pl.ds(2 + x, slots)
                    change = noise[16 * slots * i : 16 * slots * (i + 1), 128 * part : 128 * part + 128]
                    before = ext[step, tile, place, own_rows]
                    ext[step + 1, tile, place, own_rows] = before + delta * change.reshape(slots, 16, 128)

        for half in range(2):
            update(noise_of(half, 2, 10, 6), half, (2, 8), 6)

        def side_slot(x, to, keep):
            for tile in range(TILES):
                value = ext[step, tile, x + 2]
                if tile >= 4:
                    value = value * on_z
                if keep is not None:
                    value = value * keep
                for tap, rows in enumerate(three_rows(value)):
                    taps_side[tap, to, :, lanes_of(tile)] = rows.astype(BF16)

        for to, x in ((2, 0), (3, 1), (4, 14), (5, 15)):
            side_slot(x, to, None)
        for copy in copies(step, (-1, 1)):
            copy.wait_recv()
        for to, x in ((0, -2), (1, -1), (6, 16), (7, 17)):
            side_slot(x, to, on_x)

        keep_low = jnp.where(row8 < 2, on_x, 1.0)
        keep_high = jnp.where(row8 >= 6, on_x, 1.0)
        for tap_y in range(3):
            for tile in range(TILES):
                scale = on_z if tile >= 4 else 1.0
                for i, row in enumerate(((22 + tap_y) % 24, 15 + tap_y)):
                    first = flat[tile, pl.ds(row, 8, stride=YS), :] * (keep_low * scale)
                    last = flat[tile, pl.ds(12 * YS + row, 8, stride=YS), :] * (keep_high * scale)
                    for tap_x in range(3):
                        pair = [pltpu.roll(part, 8 - tap_x, 0) if tap_x else part for part in (first, last)]
                        rows = jnp.concatenate(pair, axis=0).astype(BF16)
                        edge_side[3 * tap_x + tap_y, pl.ds(16 * i, 16), lanes_of(tile)] = rows

        def side_inputs(tiles):
            columns = []
            for tap_x in range(3):
                for tap_y in range(3):
                    for tile in tiles:
                        columns.append(jnp.concatenate([
                            taps_side[tap_y, pl.ds(tap_x, 2), :, lanes_of(tile)].reshape(32, 128),
                            taps_side[tap_y, pl.ds(4 + tap_x, 2), :, lanes_of(tile)].reshape(32, 128),
                            edge_side[3 * tap_x + tap_y, :, lanes_of(tile)],
                        ], axis=0))
            return jnp.concatenate(columns, axis=1)

        def keep_side(total, tile):
            value = silu(total, tile)
            for i, slot in enumerate((0, 1, 16, 17)):
                hidden[tile, slot, own_rows] = value[16 * i : 16 * i + 16]
            for i, row in enumerate((23, 16)):
                for at, slot in ((0, 0), (1, 1), (12, 16), (13, 17)):
                    place = 64 + 16 * i + at
                    hidden[tile, slot, pl.ds(row, 1)] = value[place : place + 1]

        total = jnp.dot(side_inputs((5, 0, 1)), w1[0].reshape(3456, 256), preferred_element_type=F32)
        keep_side(total[:, :128], 0)
        keep_side(total[:, 128:], 1)
        total = jnp.dot(side_inputs((1, 2, 3)), w1[flag_z].reshape(3456, 256), preferred_element_type=F32)
        keep_side(total[:, :128], 2)
        keep_side(total[:, 128:], 3)
        total = jnp.dot(side_inputs((3, 4)), w1c[...].reshape(2304, 128), preferred_element_type=F32)
        keep_side(total, 4)
        hidden_slot(0, 0, on_x)
        hidden_slot(1, 1, None)
        hidden_slot(16, 18, None)
        hidden_slot(17, 19, on_x)
        for half in range(2):
            update(noise_of(half, 0, 16, 2), half, (0, 14), 2)

        @pl.when(step + 1 < steps)
        def _():
            for copy in copies(step + 1):
                copy.start()

        return carry

    lax.fori_loop(0, steps, step_body, 0)

    stores = [
        pltpu.make_async_copy(
            ext.at[steps, tile, pl.ds(2, 16), pl.ds(0, 16)],
            out_ref.at[:, :, pl.ds(128 * tile, 128)],
            load_sem.at[tile],
        )
        for tile in range(4)
    ]
    for store in stores:
        store.start()

    def drain(step, carry):
        for copy in copies(step):
            copy.wait_send()
        return carry

    lax.fori_loop(0, steps, drain, 0)
    for store in stores:
        store.wait()


def time_bias(timesteps, time_weight):
    half_c = time_weight.shape[0] // 2
    freqs = jnp.exp(-math.log(10000.0) * jnp.arange(half_c, dtype=F32) / half_c)
    angles = timesteps.astype(F32)[:, None] * freqs
    emb = jnp.concatenate([jnp.sin(angles), jnp.cos(angles)], axis=1)
    return jnp.dot(emb, time_weight, precision=lax.Precision.HIGHEST)


def shards(latent, conv_first, conv_second, time_weight, timesteps, offsets):
    steps = timesteps.shape[0]
    bias = time_bias(timesteps, time_weight)
    bias = jnp.concatenate([bias, bias], axis=1).reshape(steps, 1, 128)
    later = jnp.concatenate([timesteps[1:], jnp.zeros((1,), jnp.int32)])
    delta = (later - timesteps).astype(F32) / 1000.0
    vmem = pl.BlockSpec(memory_space=pltpu.VMEM)
    smem = pl.BlockSpec(memory_space=pltpu.SMEM)
    anywhere = pl.BlockSpec(memory_space=pl.ANY)
    count = len(DIRECTIONS)

    def body(*refs):
        kernel(steps, *refs)

    return pl.pallas_call(
        body,
        out_shape=jax.ShapeDtypeStruct(latent.shape, latent.dtype),
        in_specs=[anywhere, vmem, vmem, vmem, smem, smem],
        out_specs=anywhere,
        scratch_shapes=[
            pltpu.VMEM((steps + 1, TILES, XS, YS, 128), F32),
            pltpu.VMEM((2, 9, 384, 256), BF16),
            pltpu.VMEM((9, 256, 128), BF16),
            pltpu.VMEM((9, 384, 256), BF16),
            pltpu.VMEM((3, 18, 16, 768), BF16),
            pltpu.VMEM((3, 8, 16, 768), BF16),
            pltpu.VMEM((3, 8, 16, 768), BF16),
            pltpu.VMEM((9, 32, 768), BF16),
            pltpu.VMEM((5, 224, 128), F32),
            pltpu.VMEM((5, 18, YS, 128), F32),
            pltpu.VMEM((3, 20, 16, 768), BF16),
            pltpu.SemaphoreType.DMA((steps, count)),
            pltpu.SemaphoreType.DMA((steps, count)),
            pltpu.SemaphoreType.DMA((4,)),
        ],
        compiler_params=pltpu.CompilerParams(
            collective_id=0, has_side_effects=True, vmem_limit_bytes=48 * 2**20
        ),
    )(latent, conv_first.reshape(9, 192, 64), conv_second.reshape(9, 192, 64), bias, delta, offsets)


def solution(mesh):
    return jax.shard_map(
        shards,
        mesh=mesh,
        in_specs=(P("gx", "gy", "gz"), P(), P(), P(), P(), P()),
        out_specs=P("gx", "gy", "gz"),
        check_vma=False,
    )
```

```python
import itertools
import math

import jax
import jax.numpy as jnp
from jax import lax
from jax.experimental import pallas as pl
from jax.experimental.pallas import tpu as pltpu
from jax.sharding import PartitionSpec as P

MESH = pl.DeviceIdType.MESH
F32 = jnp.float32
BF16 = jnp.bfloat16

XS, YS, TILES = 20, 24, 6


def directions():
    every = [d for d in itertools.product((-1, 0, 1), repeat=3) if d != (0, 0, 0)]
    return sorted(every, key=lambda d: (d[0] != 0, -sum(map(abs, d))))


DIRECTIONS = directions()


WHOLE, INNER, SIDES = pl.ds(0, 16), pl.ds(0, 12), pl.ds(12, 4)


def slot_of(x):
    return (x - 2) % 16 if 0 <= x < 16 else x if x >= 16 else x + 20


def sent(d, part):
    x = {-1: pl.ds(14, 2), 0: part, 1: pl.ds(12, 2)}[d[0]]
    y = {-1: pl.ds(0, 2), 0: pl.ds(0, 16), 1: pl.ds(14, 2)}[d[1]]
    z = {-1: pl.ds(0, 1), 0: pl.ds(0, 4), 1: pl.ds(3, 1)}[d[2]]
    return z, x, y


def landed(d, part):
    x = {-1: pl.ds(16, 2), 0: part, 1: pl.ds(18, 2)}[d[0]]
    y = {-1: pl.ds(16, 2), 0: pl.ds(0, 16), 1: pl.ds(22, 2)}[d[1]]
    z = {-1: pl.ds(4, 1), 0: pl.ds(0, 4), 1: pl.ds(5, 1)}[d[2]]
    return z, x, y


def neighbour(d):
    place = []
    for name, by in zip(("gx", "gy", "gz"), d):
        size = lax.axis_size(name)
        place.append(lax.rem(lax.axis_index(name) + by + size, size))
    return tuple(place)


def kernel(
    steps, latent_ref, first_ref, second_ref, bias_ref, delta_ref, offsets_ref, out_ref,
    ext, w1, w1c, w2, taps_in, edge_in, taps_side, edge_side, partial, hidden, taps_hid, send_sem, recv_sem, load_sem,
):
    loads = [
        pltpu.make_async_copy(
            latent_ref.at[pl.ds(x, count), :, pl.ds(128 * tile, 128)],
            ext.at[0, tile, pl.ds(slot_of(x), count), pl.ds(0, 16)],
            load_sem.at[tile, i],
        )
        for tile in range(4)
        for i, (x, count) in enumerate(((2, 14), (0, 2)))
    ]
    for load in loads:
        load.start()
    barrier = pltpu.get_barrier_semaphore()
    for d in DIRECTIONS:
        pl.semaphore_signal(barrier, inc=1, device_id=neighbour(d), device_id_type=MESH)
    pl.semaphore_wait(barrier, len(DIRECTIONS))
    for load in loads:
        load.wait()

    def copies(step, sides=(-1, 0, 1), part=WHOLE, heights=(-1, 0, 1)):
        return [
            pltpu.make_async_remote_copy(
                src_ref=ext.at[(step, *sent(d, part))],
                dst_ref=ext.at[(step, *landed(d, part))],
                send_sem=send_sem.at[step, i],
                recv_sem=recv_sem.at[step, i],
                device_id=neighbour(d),
                device_id_type=MESH,
            )
            for i, d in enumerate(DIRECTIONS)
            if d[0] in sides and d[2] in heights
        ]

    for copy in copies(0):
        copy.start()

    w1[...] = jnp.zeros_like(w1)
    w1c[...] = jnp.zeros_like(w1c)
    w2[...] = jnp.zeros_like(w2)

    def place_weights(tap, carry):
        one = first_ref[tap]
        two = second_ref[tap]
        for out in range(4):
            rows = pl.ds(out * 64, 192)
            lanes = pl.ds(out * 64, 64)
            w1[0, tap, rows, lanes] = one
            w2[tap, rows, lanes] = two
            if out < 2:
                w1c[tap, rows, lanes] = one
        w1[1, tap, pl.ds(0, 128), pl.ds(0, 64)] = one[:128]
        w1[1, tap, pl.ds(128, 128), pl.ds(64, 64)] = one[64:]
        w1[1, tap, pl.ds(128, 192), pl.ds(128, 64)] = one
        w1[1, tap, pl.ds(192, 192), pl.ds(192, 64)] = one
        return carry

    lax.fori_loop(0, 9, place_weights, 0)

    row8 = lax.broadcasted_iota(jnp.int32, (8, 128), 0)
    row16 = lax.broadcasted_iota(jnp.int32, (16, 128), 0)
    lane128 = lax.broadcasted_iota(jnp.int32, (1, 128), 1)
    own_rows = pl.ds(0, 16)

    def step_body(step, carry):
        flag_x = offsets_ref[step, 0]
        flag_y = offsets_ref[step, 1]
        flag_z = offsets_ref[step, 2]
        on_x = flag_x.astype(F32)
        on_y = flag_y.astype(F32)
        on_z = flag_z.astype(F32)
        off_x = 1.0 - on_x
        cut_down = row16 == 8 * flag_y
        cut_up = row16 == 15 - 8 * flag_y
        cut_back = jnp.logical_and(row16 == 6, flag_x == 1)
        cut_ahead = jnp.logical_and(row16 == 5, flag_x == 1)
        bias = bias_ref[step]
        delta = delta_ref[step]
        flat = ext.at[step].reshape(TILES, XS * YS, 128)
        flat_hidden = hidden.reshape(5, 18 * YS, 128)

        def three_rows(value):
            count = value.shape[0]
            down = pltpu.roll(value, 1, 0)[:16]
            up = pltpu.roll(value, count - 1, 0)[:16]
            return jnp.where(cut_down, 0.0, down), value[:16], jnp.where(cut_up, 0.0, up)

        def lanes_of(tile):
            return pl.ds(128 * tile, 128)

        def close_gap(taps, gap, tiles):
            lanes = pl.ds(128 * tiles[0], 128 * len(tiles))
            for tap in range(3):
                taps[tap, gap, :, lanes] = (taps[tap, gap + 2, :, lanes].astype(F32) * off_x).astype(BF16)
                taps[tap, gap + 1, :, lanes] = (taps[tap, gap - 1, :, lanes].astype(F32) * off_x).astype(BF16)

        def input_slots(tiles, keep):
            def one(x, carry):
                to = x + 2 * (x >= 8).astype(jnp.int32)
                for tile in tiles:
                    value = ext[step, tile, lax.rem(x + 14, 16), own_rows]
                    if keep is not None:
                        value = value * keep
                    for tap, rows in enumerate(three_rows(value)):
                        taps_in[tap, to, :, lanes_of(tile)] = rows.astype(BF16)
                return carry

            lax.fori_loop(0, 16, one, 0)
            close_gap(taps_in, 8, tiles)

        def inner_inputs(tiles):
            columns = []
            for tap_x in range(3):
                for tap_y in range(3):
                    for tile in tiles:
                        columns.append(jnp.concatenate([
                            taps_in[tap_y, pl.ds(tap_x, 7), :, lanes_of(tile)].reshape(112, 128),
                            taps_in[tap_y, pl.ds(9 + tap_x, 7), :, lanes_of(tile)].reshape(112, 128),
                        ], axis=0))
            return jnp.concatenate(columns, axis=1)

        def silu(total, tile):
            value = total + bias
            value = value / (1.0 + jnp.exp(-value))
            if tile == 0:
                value = value * jnp.where(lane128 < 64, on_z, 1.0)
            if tile == 4:
                value = value * jnp.where(lane128 >= 64, on_z, 1.0)
            return value

        input_slots((0, 1, 2, 3), None)
        total = jnp.dot(
            inner_inputs((0, 1)), w1[0, :, pl.ds(128, 256), :].reshape(2304, 256), preferred_element_type=F32
        )
        partial[0] = total[:, :128]
        partial[1] = total[:, 128:]
        total = jnp.dot(inner_inputs((1, 2, 3)), w1[flag_z].reshape(3456, 256), preferred_element_type=F32)
        partial[2] = total[:, :128]
        partial[3] = total[:, 128:]
        partial[4] = jnp.dot(
            inner_inputs((3,)), w1c[:, pl.ds(0, 128), :].reshape(1152, 128), preferred_element_type=F32
        )

        for copy in copies(step, (0,)):
            copy.wait_recv()
        input_slots((4, 5), on_z)

        for place, row in enumerate((22, 23, 0, 1, 14, 15, 16, 17)):
            keep_row = on_y if row >= 16 else None
            for tile in range(TILES):
                value = flat[tile, pl.ds(row, 16, stride=YS), :]
                if keep_row is not None:
                    value = value * keep_row
                if tile >= 4:
                    value = value * on_z
                back = jnp.where(cut_back, 0.0, pltpu.roll(value, 1, 0))
                ahead = jnp.where(cut_ahead, 0.0, pltpu.roll(value, 15, 0))
                for tap, rows in enumerate((back, value, ahead)):
                    edge_in[tap, place, :, lanes_of(tile)] = rows.astype(BF16)

        def edge_inputs(tiles):
            columns = []
            for tap_x in range(3):
                for tap_y in range(3):
                    for tile in tiles:
                        columns.append(jnp.concatenate([
                            edge_in[tap_x, pl.ds(tap_y, 2), :, lanes_of(tile)].reshape(32, 128),
                            edge_in[tap_x, pl.ds(4 + tap_y, 2), :, lanes_of(tile)].reshape(32, 128),
                        ], axis=0))
            return jnp.concatenate(columns, axis=1)

        def keep_inner(total, tile):
            value = silu(total, tile)
            for x in range(1, 15):
                hidden[tile, slot_of(x), own_rows] = value[16 * x - 16 : 16 * x]

        def keep_edges(total, tile):
            value = silu(total, tile)
            for i, row in enumerate((23, 0, 15, 16)):
                flat_hidden[tile, pl.ds(row, 16, stride=YS), :] = value[16 * i : 16 * i + 16]

        total = jnp.dot(
            inner_inputs((5,)), w1[0, :, pl.ds(0, 128), :].reshape(1152, 256), preferred_element_type=F32
        )
        keep_inner(partial[0] + total[:, :128], 0)
        keep_inner(partial[1] + total[:, 128:], 1)
        keep_inner(partial[2], 2)
        keep_inner(partial[3], 3)
        total = jnp.dot(
            inner_inputs((4,)), w1c[:, pl.ds(128, 128), :].reshape(1152, 128), preferred_element_type=F32
        )
        keep_inner(partial[4] + total, 4)
        total = jnp.dot(edge_inputs((5, 0, 1)), w1[0].reshape(3456, 256), preferred_element_type=F32)
        keep_edges(total[:, :128], 0)
        keep_edges(total[:, 128:], 1)
        total = jnp.dot(edge_inputs((1, 2, 3)), w1[flag_z].reshape(3456, 256), preferred_element_type=F32)
        keep_edges(total[:, :128], 2)
        keep_edges(total[:, 128:], 3)
        total = jnp.dot(edge_inputs((3, 4)), w1c[...].reshape(2304, 128), preferred_element_type=F32)
        keep_edges(total, 4)

        low = jnp.where(lane128 < 64, 1.0, 1.0 - on_z)
        high = jnp.where(lane128 >= 64, 1.0, 1.0 - on_z)

        def hidden_slot(slot, to, keep_x):
            sources = ((0, None), (1, None), (2, low), (2, high), (3, None), (4, None))
            for place, (tile, keep) in enumerate(sources):
                value = hidden[tile, slot]
                if keep is not None:
                    value = value * keep
                if keep_x is not None:
                    value = value * keep_x
                for tap, rows in enumerate(three_rows(value)):
                    taps_hid[tap, to, :, lanes_of(place)] = rows.astype(BF16)

        def inner_slot(x, carry):
            hidden_slot(lax.rem(x + 14, 16), x + 1 + 2 * (x >= 8).astype(jnp.int32), None)
            return carry

        lax.fori_loop(1, 15, inner_slot, 0)
        close_gap(taps_hid, 9, tuple(range(6)))

        def noise_of(half, low_slot, high_slot, slots):
            lanes = pl.ds(384 * half, 384)
            columns = []
            for tap_x in range(3):
                for tap_y in range(3):
                    columns.append(jnp.concatenate([
                        taps_hid[tap_y, pl.ds(start + tap_x, slots), :, lanes].reshape(16 * slots, 384)
                        for start in (low_slot, high_slot)
                    ], axis=0))
            values = jnp.concatenate(columns, axis=1)
            return jnp.dot(values, w2[...].reshape(3456, 256), preferred_element_type=F32)

        def update(noise, half, starts, slots):
            for part in range(2):
                tile = 2 * half + part
                for i, x in enumerate(starts):
                    place = pl.ds(slot_of(x), slots)
                    change = noise[16 * slots * i : 16 * slots * (i + 1), 128 * part : 128 * part + 128]
                    before = ext[step, tile, place, own_rows]
                    ext[step + 1, tile, place, own_rows] = before + delta * change.reshape(slots, 16, 128)

        for half in range(2):
            update(noise_of(half, 2, 10, 6), half, (2, 8), 6)

        @pl.when(step + 1 < steps)
        def _():
            for copy in copies(step + 1, (0,), INNER):
                copy.start()

        def side_slot(x, to, keep):
            for tile in range(TILES):
                value = ext[step, tile, slot_of(x)]
                if tile >= 4:
                    value = value * on_z
                if keep is not None:
                    value = value * keep
                for tap, rows in enumerate(three_rows(value)):
                    taps_side[tap, to, :, lanes_of(tile)] = rows.astype(BF16)

        for to, x in ((2, 0), (3, 1), (4, 14), (5, 15)):
            side_slot(x, to, None)
        for copy in copies(step, (-1, 1)):
            copy.wait_recv()
        for to, x in ((0, -2), (1, -1), (6, 16), (7, 17)):
            side_slot(x, to, on_x)

        keep_sides = jnp.where(row8 >= 4, on_x, 1.0)
        for tap_y in range(3):
            for tile in range(TILES):
                scale = on_z if tile >= 4 else 1.0
                for i, row in enumerate(((22 + tap_y) % 24, 15 + tap_y)):
                    value = flat[tile, pl.ds(12 * YS + row, 8, stride=YS), :] * (keep_sides * scale)
                    first = jnp.where(row8 < 2, pltpu.roll(value, 2, 0), value)
                    last = jnp.where(row8 < 2, value, pltpu.roll(value, 6, 0))
                    for tap_x in range(3):
                        pair = [pltpu.roll(part, 8 - tap_x, 0) if tap_x else part for part in (first, last)]
                        rows = jnp.concatenate(pair, axis=0).astype(BF16)
                        edge_side[3 * tap_x + tap_y, pl.ds(16 * i, 16), lanes_of(tile)] = rows

        def side_inputs(tiles):
            columns = []
            for tap_x in range(3):
                for tap_y in range(3):
                    for tile in tiles:
                        columns.append(jnp.concatenate([
                            taps_side[tap_y, pl.ds(tap_x, 2), :, lanes_of(tile)].reshape(32, 128),
                            taps_side[tap_y, pl.ds(4 + tap_x, 2), :, lanes_of(tile)].reshape(32, 128),
                            edge_side[3 * tap_x + tap_y, :, lanes_of(tile)],
                        ], axis=0))
            return jnp.concatenate(columns, axis=1)

        def keep_side(total, tile):
            value = silu(total, tile)
            for i, slot in enumerate((17, 14, 13, 16)):
                hidden[tile, slot, own_rows] = value[16 * i : 16 * i + 16]
            for i, row in enumerate((23, 16)):
                for at, slot in ((0, 17), (1, 14), (8, 13), (9, 16)):
                    place = 64 + 16 * i + at
                    hidden[tile, slot, pl.ds(row, 1)] = value[place : place + 1]

        total = jnp.dot(side_inputs((5, 0, 1)), w1[0].reshape(3456, 256), preferred_element_type=F32)
        keep_side(total[:, :128], 0)
        keep_side(total[:, 128:], 1)
        total = jnp.dot(side_inputs((1, 2, 3)), w1[flag_z].reshape(3456, 256), preferred_element_type=F32)
        keep_side(total[:, :128], 2)
        keep_side(total[:, 128:], 3)
        total = jnp.dot(side_inputs((3, 4)), w1c[...].reshape(2304, 128), preferred_element_type=F32)
        keep_side(total, 4)
        hidden_slot(17, 0, on_x)
        hidden_slot(14, 1, None)
        hidden_slot(13, 18, None)
        hidden_slot(16, 19, on_x)
        for half in range(2):
            update(noise_of(half, 0, 16, 2), half, (0, 14), 2)

            @pl.when(step + 1 < steps)
            def _():
                if half:
                    for copy in copies(step + 1, (0,), SIDES) + copies(step + 1, (-1, 1)):
                        copy.start()

        return carry

    lax.fori_loop(0, steps, step_body, 0)

    stores = [
        pltpu.make_async_copy(
            ext.at[steps, tile, pl.ds(slot_of(x), count), pl.ds(0, 16)],
            out_ref.at[pl.ds(x, count), :, pl.ds(128 * tile, 128)],
            load_sem.at[tile, i],
        )
        for tile in range(4)
        for i, (x, count) in enumerate(((2, 14), (0, 2)))
    ]
    for store in stores:
        store.start()

    def drain(step, carry):
        for copy in copies(step):
            copy.wait_send()
        return carry

    lax.fori_loop(0, steps, drain, 0)
    for store in stores:
        store.wait()


def time_bias(timesteps, time_weight):
    half_c = time_weight.shape[0] // 2
    freqs = jnp.exp(-math.log(10000.0) * jnp.arange(half_c, dtype=F32) / half_c)
    angles = timesteps.astype(F32)[:, None] * freqs
    emb = jnp.concatenate([jnp.sin(angles), jnp.cos(angles)], axis=1)
    return jnp.dot(emb, time_weight, precision=lax.Precision.HIGHEST)


def shards(latent, conv_first, conv_second, time_weight, timesteps, offsets):
    steps = timesteps.shape[0]
    bias = time_bias(timesteps, time_weight)
    bias = jnp.concatenate([bias, bias], axis=1).reshape(steps, 1, 128)
    later = jnp.concatenate([timesteps[1:], jnp.zeros((1,), jnp.int32)])
    delta = (later - timesteps).astype(F32) / 1000.0
    vmem = pl.BlockSpec(memory_space=pltpu.VMEM)
    smem = pl.BlockSpec(memory_space=pltpu.SMEM)
    anywhere = pl.BlockSpec(memory_space=pl.ANY)
    count = len(DIRECTIONS)

    def body(*refs):
        kernel(steps, *refs)

    return pl.pallas_call(
        body,
        out_shape=jax.ShapeDtypeStruct(latent.shape, latent.dtype),
        in_specs=[anywhere, vmem, vmem, vmem, smem, smem],
        out_specs=anywhere,
        scratch_shapes=[
            pltpu.VMEM((steps + 1, TILES, XS, YS, 128), F32),
            pltpu.VMEM((2, 9, 384, 256), BF16),
            pltpu.VMEM((9, 256, 128), BF16),
            pltpu.VMEM((9, 384, 256), BF16),
            pltpu.VMEM((3, 18, 16, 768), BF16),
            pltpu.VMEM((3, 8, 16, 768), BF16),
            pltpu.VMEM((3, 8, 16, 768), BF16),
            pltpu.VMEM((9, 32, 768), BF16),
            pltpu.VMEM((5, 224, 128), F32),
            pltpu.VMEM((5, 18, YS, 128), F32),
            pltpu.VMEM((3, 20, 16, 768), BF16),
            pltpu.SemaphoreType.DMA((steps, count)),
            pltpu.SemaphoreType.DMA((steps, count)),
            pltpu.SemaphoreType.DMA((4, 2)),
        ],
        compiler_params=pltpu.CompilerParams(
            collective_id=0, has_side_effects=True, vmem_limit_bytes=48 * 2**20
        ),
    )(latent, conv_first.reshape(9, 192, 64), conv_second.reshape(9, 192, 64), bias, delta, offsets)


def solution(mesh):
    return jax.shard_map(
        shards,
        mesh=mesh,
        in_specs=(P("gx", "gy", "gz"), P(), P(), P(), P(), P()),
        out_specs=P("gx", "gy", "gz"),
        check_vma=False,
    )
```

```python
import itertools
import math

import jax
import jax.numpy as jnp
from jax import lax
from jax.experimental import pallas as pl
from jax.experimental.pallas import tpu as pltpu
from jax.sharding import PartitionSpec as P

MESH = pl.DeviceIdType.MESH
F32 = jnp.float32
BF16 = jnp.bfloat16

XS, YS, TILES = 20, 24, 6


def directions():
    every = [d for d in itertools.product((-1, 0, 1), repeat=3) if d != (0, 0, 0)]
    return sorted(every, key=lambda d: (d[0] != 0, -sum(map(abs, d))))


DIRECTIONS = directions()


WHOLE, INNER, SIDES = pl.ds(0, 16), pl.ds(0, 12), pl.ds(12, 4)


def slot_of(x):
    return (x - 2) % 16 if 0 <= x < 16 else x if x >= 16 else x + 20


def sent(d, part):
    x = {-1: pl.ds(14, 2), 0: part, 1: pl.ds(12, 2)}[d[0]]
    y = {-1: pl.ds(0, 2), 0: pl.ds(0, 16), 1: pl.ds(14, 2)}[d[1]]
    z = {-1: pl.ds(0, 1), 0: pl.ds(0, 4), 1: pl.ds(3, 1)}[d[2]]
    return z, x, y


def landed(d, part):
    x = {-1: pl.ds(16, 2), 0: part, 1: pl.ds(18, 2)}[d[0]]
    y = {-1: pl.ds(16, 2), 0: pl.ds(0, 16), 1: pl.ds(22, 2)}[d[1]]
    z = {-1: pl.ds(4, 1), 0: pl.ds(0, 4), 1: pl.ds(5, 1)}[d[2]]
    return z, x, y


def neighbour(d):
    place = []
    for name, by in zip(("gx", "gy", "gz"), d):
        size = lax.axis_size(name)
        place.append(lax.rem(lax.axis_index(name) + by + size, size))
    return tuple(place)


def kernel(
    steps, latent_ref, first_hbm, second_hbm, time_hbm, timesteps_hbm, offsets_hbm, out_ref,
    first_ref, second_ref, time_ref, timesteps_ref, offsets_ref, ext, bias_ref, w1, w1c, w2, taps_in, edge_in, taps_side, edge_side, partial, hidden, taps_hid, send_sem, recv_sem, load_sem, small_sem,
):
    barrier = pltpu.get_barrier_semaphore()
    for d in DIRECTIONS:
        pl.semaphore_signal(barrier, inc=1, device_id=neighbour(d), device_id_type=MESH)
    loads = [
        pltpu.make_async_copy(
            latent_ref.at[pl.ds(x, count), :, pl.ds(128 * tile, 128)],
            ext.at[0, tile, pl.ds(slot_of(x), count), pl.ds(0, 16)],
            load_sem.at[tile, i],
        )
        for tile in range(4)
        for i, (x, count) in enumerate(((2, 14), (0, 2)))
    ]
    small = [
        pltpu.make_async_copy(source, target, small_sem.at[i])
        for i, (source, target) in enumerate((
            (first_hbm, first_ref), (second_hbm, second_ref), (time_hbm, time_ref),
            (timesteps_hbm, timesteps_ref), (offsets_hbm, offsets_ref),
        ))
    ]
    for load in loads + small:
        load.start()
    pl.semaphore_wait(barrier, len(DIRECTIONS))
    for load in loads:
        load.wait()

    def copies(step, sides=(-1, 0, 1), part=WHOLE, heights=(-1, 0, 1)):
        return [
            pltpu.make_async_remote_copy(
                src_ref=ext.at[(step, *sent(d, part))],
                dst_ref=ext.at[(step, *landed(d, part))],
                send_sem=send_sem.at[step, i],
                recv_sem=recv_sem.at[step, i],
                device_id=neighbour(d),
                device_id_type=MESH,
            )
            for i, d in enumerate(DIRECTIONS)
            if d[0] in sides and d[2] in heights
        ]

    for copy in copies(0):
        copy.start()

    for load in small:
        load.wait()
    w1[...] = jnp.zeros_like(w1)
    w1c[...] = jnp.zeros_like(w1c)
    w2[...] = jnp.zeros_like(w2)

    def place_weights(tap, carry):
        one = first_ref[tap].T
        two = second_ref[tap].T
        for out in range(4):
            rows = pl.ds(out * 64, 192)
            lanes = pl.ds(out * 64, 64)
            w1[0, tap, rows, lanes] = one
            w2[tap, rows, lanes] = two
            if out < 2:
                w1c[tap, rows, lanes] = one
        w1[1, tap, pl.ds(0, 128), pl.ds(0, 64)] = one[:128]
        w1[1, tap, pl.ds(128, 128), pl.ds(64, 64)] = one[64:]
        w1[1, tap, pl.ds(128, 192), pl.ds(128, 64)] = one
        w1[1, tap, pl.ds(192, 192), pl.ds(192, 64)] = one
        return carry

    lax.fori_loop(0, 9, place_weights, 0)

    entry = lax.broadcasted_iota(jnp.int32, (64, 128), 0)
    lane = lax.broadcasted_iota(jnp.int32, (64, 128), 1)
    order = jnp.where(entry < 32, entry, entry - 32).astype(F32)
    angles = jnp.zeros((64, 128), F32)
    for step in range(steps):
        angles = jnp.where(lane == step, timesteps_ref[step].astype(F32), angles)
    angles = angles * jnp.exp(-math.log(10000.0) * order / 32)
    embedding = jnp.where(entry < 32, jnp.sin(angles), jnp.cos(angles))
    time_weight = time_ref[...]
    for step in range(steps):
        bias = jnp.sum(embedding[:, step : step + 1] * time_weight, axis=0, keepdims=True)
        bias_ref[step, :, pl.ds(0, 64)] = bias
        bias_ref[step, :, pl.ds(64, 64)] = bias

    row8 = lax.broadcasted_iota(jnp.int32, (8, 128), 0)
    row16 = lax.broadcasted_iota(jnp.int32, (16, 128), 0)
    lane128 = lax.broadcasted_iota(jnp.int32, (1, 128), 1)
    own_rows = pl.ds(0, 16)

    def step_body(step, carry):
        flag_x = offsets_ref[step, 0]
        flag_y = offsets_ref[step, 1]
        flag_z = offsets_ref[step, 2]
        on_x = flag_x.astype(F32)
        on_y = flag_y.astype(F32)
        on_z = flag_z.astype(F32)
        off_x = 1.0 - on_x
        cut_down = row16 == 8 * flag_y
        cut_up = row16 == 15 - 8 * flag_y
        cut_back = jnp.logical_and(row16 == 6, flag_x == 1)
        cut_ahead = jnp.logical_and(row16 == 5, flag_x == 1)
        bias = bias_ref[step]
        later = jnp.where(step + 1 < steps, timesteps_ref[jnp.minimum(step + 1, steps - 1)], 0)
        delta = jnp.full((1, 1, 128), (later - timesteps_ref[step]).astype(F32)) / 1000.0
        flat = ext.at[step].reshape(TILES, XS * YS, 128)
        flat_hidden = hidden.reshape(5, 18 * YS, 128)

        def three_rows(value):
            count = value.shape[0]
            down = pltpu.roll(value, 1, 0)[:16]
            up = pltpu.roll(value, count - 1, 0)[:16]
            return jnp.where(cut_down, 0.0, down), value[:16], jnp.where(cut_up, 0.0, up)

        def lanes_of(tile):
            return pl.ds(128 * tile, 128)

        def close_gap(taps, gap, tiles):
            lanes = pl.ds(128 * tiles[0], 128 * len(tiles))
            for tap in range(3):
                taps[tap, gap, :, lanes] = (taps[tap, gap + 2, :, lanes].astype(F32) * off_x).astype(BF16)
                taps[tap, gap + 1, :, lanes] = (taps[tap, gap - 1, :, lanes].astype(F32) * off_x).astype(BF16)

        def input_slots(tiles, keep):
            def one(x, carry):
                to = x + 2 * (x >= 8).astype(jnp.int32)
                for tile in tiles:
                    value = ext[step, tile, lax.rem(x + 14, 16), own_rows]
                    if keep is not None:
                        value = value * keep
                    for tap, rows in enumerate(three_rows(value)):
                        taps_in[tap, to, :, lanes_of(tile)] = rows.astype(BF16)
                return carry

            lax.fori_loop(0, 16, one, 0)
            close_gap(taps_in, 8, tiles)

        def inner_inputs(tiles):
            columns = []
            for tap_x in range(3):
                for tap_y in range(3):
                    for tile in tiles:
                        columns.append(jnp.concatenate([
                            taps_in[tap_y, pl.ds(tap_x, 7), :, lanes_of(tile)].reshape(112, 128),
                            taps_in[tap_y, pl.ds(9 + tap_x, 7), :, lanes_of(tile)].reshape(112, 128),
                        ], axis=0))
            return jnp.concatenate(columns, axis=1)

        def silu(total, tile):
            value = total + bias
            value = value / (1.0 + jnp.exp(-value))
            if tile == 0:
                value = value * jnp.where(lane128 < 64, on_z, 1.0)
            if tile == 4:
                value = value * jnp.where(lane128 >= 64, on_z, 1.0)
            return value

        input_slots((0, 1, 2, 3), None)
        total = jnp.dot(
            inner_inputs((0, 1)), w1[0, :, pl.ds(128, 256), :].reshape(2304, 256), preferred_element_type=F32
        )
        partial[0] = total[:, :128]
        partial[1] = total[:, 128:]
        total = jnp.dot(inner_inputs((1, 2, 3)), w1[flag_z].reshape(3456, 256), preferred_element_type=F32)
        partial[2] = total[:, :128]
        partial[3] = total[:, 128:]
        partial[4] = jnp.dot(
            inner_inputs((3,)), w1c[:, pl.ds(0, 128), :].reshape(1152, 128), preferred_element_type=F32
        )

        for copy in copies(step, (0,)):
            copy.wait_recv()
        input_slots((4, 5), on_z)

        for place, row in enumerate((22, 23, 0, 1, 14, 15, 16, 17)):
            keep_row = on_y if row >= 16 else None
            for tile in range(TILES):
                value = flat[tile, pl.ds(row, 16, stride=YS), :]
                if keep_row is not None:
                    value = value * keep_row
                if tile >= 4:
                    value = value * on_z
                back = jnp.where(cut_back, 0.0, pltpu.roll(value, 1, 0))
                ahead = jnp.where(cut_ahead, 0.0, pltpu.roll(value, 15, 0))
                for tap, rows in enumerate((back, value, ahead)):
                    edge_in[tap, place, :, lanes_of(tile)] = rows.astype(BF16)

        def edge_inputs(tiles):
            columns = []
            for tap_x in range(3):
                for tap_y in range(3):
                    for tile in tiles:
                        columns.append(jnp.concatenate([
                            edge_in[tap_x, pl.ds(tap_y, 2), :, lanes_of(tile)].reshape(32, 128),
                            edge_in[tap_x, pl.ds(4 + tap_y, 2), :, lanes_of(tile)].reshape(32, 128),
                        ], axis=0))
            return jnp.concatenate(columns, axis=1)

        def keep_inner(total, tile):
            value = silu(total, tile)
            for x in range(1, 15):
                hidden[tile, slot_of(x), own_rows] = value[16 * x - 16 : 16 * x]

        def keep_edges(total, tile):
            value = silu(total, tile)
            for i, row in enumerate((23, 0, 15, 16)):
                flat_hidden[tile, pl.ds(row, 16, stride=YS), :] = value[16 * i : 16 * i + 16]

        total = jnp.dot(
            inner_inputs((5,)), w1[0, :, pl.ds(0, 128), :].reshape(1152, 256), preferred_element_type=F32
        )
        keep_inner(partial[0] + total[:, :128], 0)
        keep_inner(partial[1] + total[:, 128:], 1)
        keep_inner(partial[2], 2)
        keep_inner(partial[3], 3)
        total = jnp.dot(
            inner_inputs((4,)), w1c[:, pl.ds(128, 128), :].reshape(1152, 128), preferred_element_type=F32
        )
        keep_inner(partial[4] + total, 4)
        total = jnp.dot(edge_inputs((5, 0, 1)), w1[0].reshape(3456, 256), preferred_element_type=F32)
        keep_edges(total[:, :128], 0)
        keep_edges(total[:, 128:], 1)
        total = jnp.dot(edge_inputs((1, 2, 3)), w1[flag_z].reshape(3456, 256), preferred_element_type=F32)
        keep_edges(total[:, :128], 2)
        keep_edges(total[:, 128:], 3)
        total = jnp.dot(edge_inputs((3, 4)), w1c[...].reshape(2304, 128), preferred_element_type=F32)
        keep_edges(total, 4)

        low = jnp.where(lane128 < 64, 1.0, 1.0 - on_z)
        high = jnp.where(lane128 >= 64, 1.0, 1.0 - on_z)

        def hidden_slot(slot, to, keep_x):
            sources = ((0, None), (1, None), (2, low), (2, high), (3, None), (4, None))
            for place, (tile, keep) in enumerate(sources):
                value = hidden[tile, slot]
                if keep is not None:
                    value = value * keep
                if keep_x is not None:
                    value = value * keep_x
                for tap, rows in enumerate(three_rows(value)):
                    taps_hid[tap, to, :, lanes_of(place)] = rows.astype(BF16)

        def inner_slot(x, carry):
            hidden_slot(lax.rem(x + 14, 16), x + 1 + 2 * (x >= 8).astype(jnp.int32), None)
            return carry

        lax.fori_loop(1, 15, inner_slot, 0)
        close_gap(taps_hid, 9, tuple(range(6)))

        def noise_of(half, low_slot, high_slot, slots):
            lanes = pl.ds(384 * half, 384)
            columns = []
            for tap_x in range(3):
                for tap_y in range(3):
                    columns.append(jnp.concatenate([
                        taps_hid[tap_y, pl.ds(start + tap_x, slots), :, lanes].reshape(16 * slots, 384)
                        for start in (low_slot, high_slot)
                    ], axis=0))
            values = jnp.concatenate(columns, axis=1)
            return jnp.dot(values, w2[...].reshape(3456, 256), preferred_element_type=F32)

        def update(noise, half, starts, slots):
            for part in range(2):
                tile = 2 * half + part
                for i, x in enumerate(starts):
                    place = pl.ds(slot_of(x), slots)
                    change = noise[16 * slots * i : 16 * slots * (i + 1), 128 * part : 128 * part + 128]
                    before = ext[step, tile, place, own_rows]
                    ext[step + 1, tile, place, own_rows] = before + delta * change.reshape(slots, 16, 128)

        for half in range(2):
            update(noise_of(half, 2, 10, 6), half, (2, 8), 6)

        @pl.when(step + 1 < steps)
        def _():
            for copy in copies(step + 1, (0,), INNER):
                copy.start()

        def side_slot(x, to, keep):
            for tile in range(TILES):
                value = ext[step, tile, slot_of(x)]
                if tile >= 4:
                    value = value * on_z
                if keep is not None:
                    value = value * keep
                for tap, rows in enumerate(three_rows(value)):
                    taps_side[tap, to, :, lanes_of(tile)] = rows.astype(BF16)

        for to, x in ((2, 0), (3, 1), (4, 14), (5, 15)):
            side_slot(x, to, None)
        for copy in copies(step, (-1, 1)):
            copy.wait_recv()
        for to, x in ((0, -2), (1, -1), (6, 16), (7, 17)):
            side_slot(x, to, on_x)

        keep_sides = jnp.where(row8 >= 4, on_x, 1.0)
        for tap_y in range(3):
            for tile in range(TILES):
                scale = on_z if tile >= 4 else 1.0
                for i, row in enumerate(((22 + tap_y) % 24, 15 + tap_y)):
                    value = flat[tile, pl.ds(12 * YS + row, 8, stride=YS), :] * (keep_sides * scale)
                    first = jnp.where(row8 < 2, pltpu.roll(value, 2, 0), value)
                    last = jnp.where(row8 < 2, value, pltpu.roll(value, 6, 0))
                    for tap_x in range(3):
                        pair = [pltpu.roll(part, 8 - tap_x, 0) if tap_x else part for part in (first, last)]
                        rows = jnp.concatenate(pair, axis=0).astype(BF16)
                        edge_side[3 * tap_x + tap_y, pl.ds(16 * i, 16), lanes_of(tile)] = rows

        def side_inputs(tiles):
            columns = []
            for tap_x in range(3):
                for tap_y in range(3):
                    for tile in tiles:
                        columns.append(jnp.concatenate([
                            taps_side[tap_y, pl.ds(tap_x, 2), :, lanes_of(tile)].reshape(32, 128),
                            taps_side[tap_y, pl.ds(4 + tap_x, 2), :, lanes_of(tile)].reshape(32, 128),
                            edge_side[3 * tap_x + tap_y, :, lanes_of(tile)],
                        ], axis=0))
            return jnp.concatenate(columns, axis=1)

        def keep_side(total, tile):
            value = silu(total, tile)
            for i, slot in enumerate((17, 14, 13, 16)):
                hidden[tile, slot, own_rows] = value[16 * i : 16 * i + 16]
            for i, row in enumerate((23, 16)):
                for at, slot in ((0, 17), (1, 14), (8, 13), (9, 16)):
                    place = 64 + 16 * i + at
                    hidden[tile, slot, pl.ds(row, 1)] = value[place : place + 1]

        total = jnp.dot(side_inputs((5, 0, 1)), w1[0].reshape(3456, 256), preferred_element_type=F32)
        keep_side(total[:, :128], 0)
        keep_side(total[:, 128:], 1)
        total = jnp.dot(side_inputs((1, 2, 3)), w1[flag_z].reshape(3456, 256), preferred_element_type=F32)
        keep_side(total[:, :128], 2)
        keep_side(total[:, 128:], 3)
        total = jnp.dot(side_inputs((3, 4)), w1c[...].reshape(2304, 128), preferred_element_type=F32)
        keep_side(total, 4)
        hidden_slot(17, 0, on_x)
        hidden_slot(14, 1, None)
        hidden_slot(13, 18, None)
        hidden_slot(16, 19, on_x)
        for half in range(2):
            update(noise_of(half, 0, 16, 2), half, (0, 14), 2)

            @pl.when(step + 1 < steps)
            def _():
                if half:
                    for copy in copies(step + 1, (0,), SIDES) + copies(step + 1, (-1, 1)):
                        copy.start()

        return carry

    lax.fori_loop(0, steps, step_body, 0)

    stores = [
        pltpu.make_async_copy(
            ext.at[steps, tile, pl.ds(slot_of(x), count), pl.ds(0, 16)],
            out_ref.at[pl.ds(x, count), :, pl.ds(128 * tile, 128)],
            load_sem.at[tile, i],
        )
        for tile in range(4)
        for i, (x, count) in enumerate(((2, 14), (0, 2)))
    ]
    for store in stores:
        store.start()

    def drain(step, carry):
        for copy in copies(step):
            copy.wait_send()
        return carry

    lax.fori_loop(0, steps, drain, 0)
    for store in stores:
        store.wait()


def shards(latent, conv_first, conv_second, time_weight, timesteps, offsets):
    steps = timesteps.shape[0]
    first = jnp.swapaxes(conv_first, 2, 3).reshape(9, 64, 192)
    second = jnp.swapaxes(conv_second, 2, 3).reshape(9, 64, 192)
    anywhere = pl.BlockSpec(memory_space=pl.ANY)
    count = len(DIRECTIONS)

    def body(*refs):
        kernel(steps, *refs)

    return pl.pallas_call(
        body,
        out_shape=jax.ShapeDtypeStruct(latent.shape, latent.dtype),
        in_specs=[anywhere] * 6,
        out_specs=anywhere,
        scratch_shapes=[
            pltpu.VMEM(first.shape, BF16),
            pltpu.VMEM(second.shape, BF16),
            pltpu.VMEM(time_weight.shape, F32),
            pltpu.SMEM(timesteps.shape, jnp.int32),
            pltpu.SMEM(offsets.shape, jnp.int32),
            pltpu.VMEM((steps + 1, TILES, XS, YS, 128), F32),
            pltpu.VMEM((steps, 1, 128), F32),
            pltpu.VMEM((2, 9, 384, 256), BF16),
            pltpu.VMEM((9, 256, 128), BF16),
            pltpu.VMEM((9, 384, 256), BF16),
            pltpu.VMEM((3, 18, 16, 768), BF16),
            pltpu.VMEM((3, 8, 16, 768), BF16),
            pltpu.VMEM((3, 8, 16, 768), BF16),
            pltpu.VMEM((9, 32, 768), BF16),
            pltpu.VMEM((5, 224, 128), F32),
            pltpu.VMEM((5, 18, YS, 128), F32),
            pltpu.VMEM((3, 20, 16, 768), BF16),
            pltpu.SemaphoreType.DMA((steps, count)),
            pltpu.SemaphoreType.DMA((steps, count)),
            pltpu.SemaphoreType.DMA((4, 2)),
            pltpu.SemaphoreType.DMA((5,)),
        ],
        compiler_params=pltpu.CompilerParams(
            collective_id=0, has_side_effects=True, vmem_limit_bytes=60 * 2**20
        ),
    )(latent, first, second, time_weight, timesteps, offsets)


def solution(mesh):
    return jax.shard_map(
        shards,
        mesh=mesh,
        in_specs=(P("gx", "gy", "gz"), P(), P(), P(), P(), P()),
        out_specs=P("gx", "gy", "gz"),
        check_vma=False,
    )
```

```python
import itertools
import math

import jax
import jax.numpy as jnp
from jax import lax
from jax.experimental import pallas as pl
from jax.experimental.pallas import tpu as pltpu
from jax.sharding import PartitionSpec as P

MESH = pl.DeviceIdType.MESH
F32 = jnp.float32
BF16 = jnp.bfloat16

XS, YS, TILES = 20, 24, 6


def directions():
    every = [d for d in itertools.product((-1, 0, 1), repeat=3) if d != (0, 0, 0)]
    return sorted(every, key=lambda d: (d[0] != 0, -sum(map(abs, d))))


DIRECTIONS = directions()


WHOLE, INNER, SIDES = pl.ds(0, 16), pl.ds(0, 12), pl.ds(12, 4)


def slot_of(x):
    return (x - 2) % 16 if 0 <= x < 16 else x if x >= 16 else x + 20


def sent(d, part):
    x = {-1: pl.ds(14, 2), 0: part, 1: pl.ds(12, 2)}[d[0]]
    y = {-1: pl.ds(0, 2), 0: pl.ds(0, 16), 1: pl.ds(14, 2)}[d[1]]
    z = {-1: pl.ds(0, 1), 0: pl.ds(0, 4), 1: pl.ds(3, 1)}[d[2]]
    return z, x, y


def landed(d, part):
    x = {-1: pl.ds(16, 2), 0: part, 1: pl.ds(18, 2)}[d[0]]
    y = {-1: pl.ds(16, 2), 0: pl.ds(0, 16), 1: pl.ds(22, 2)}[d[1]]
    z = {-1: pl.ds(4, 1), 0: pl.ds(0, 4), 1: pl.ds(5, 1)}[d[2]]
    return z, x, y


def surroundings():
    places = []
    for name in ("gx", "gy", "gz"):
        size, me = lax.axis_size(name), lax.axis_index(name)
        places.append((lax.rem(me + size - 1, size), me, lax.rem(me + 1, size)))
    return places


def kernel(
    steps, latent_ref, first_hbm, second_hbm, time_hbm, timesteps_hbm, offsets_hbm, out_ref,
    first_ref, second_ref, time_ref, timesteps_ref, offsets_ref, ext, bias_ref, w1, w1c, w2, taps_in, edge_in, taps_side, edge_side, partial, side_partial, hidden, taps_hid, send_sem, recv_sem, load_sem, small_sem,
):
    places = surroundings()

    def neighbour(d):
        return tuple(place[by + 1] for place, by in zip(places, d))

    barrier = pltpu.get_barrier_semaphore()
    for d in DIRECTIONS:
        pl.semaphore_signal(barrier, inc=1, device_id=neighbour(d), device_id_type=MESH)
    loads = [
        pltpu.make_async_copy(
            latent_ref.at[pl.ds(x, count), :, pl.ds(128 * tile, 128)],
            ext.at[0, tile, pl.ds(slot_of(x), count), pl.ds(0, 16)],
            load_sem.at[tile, i],
        )
        for tile in range(4)
        for i, (x, count) in enumerate(((2, 14), (0, 2)))
    ]
    small = [
        pltpu.make_async_copy(source, target, small_sem.at[i])
        for i, (source, target) in enumerate((
            (first_hbm, first_ref), (second_hbm, second_ref), (time_hbm, time_ref),
            (timesteps_hbm, timesteps_ref), (offsets_hbm, offsets_ref),
        ))
    ]
    for load in loads + small:
        load.start()
    pl.semaphore_wait(barrier, len(DIRECTIONS))
    for load in loads:
        load.wait()

    def copies(step, sides=(-1, 0, 1), part=WHOLE, heights=(-1, 0, 1)):
        return [
            pltpu.make_async_remote_copy(
                src_ref=ext.at[(step, *sent(d, part))],
                dst_ref=ext.at[(step, *landed(d, part))],
                send_sem=send_sem.at[step, i],
                recv_sem=recv_sem.at[step, i],
                device_id=neighbour(d),
                device_id_type=MESH,
            )
            for i, d in enumerate(DIRECTIONS)
            if d[0] in sides and d[2] in heights
        ]

    for copy in copies(0):
        copy.start()

    for load in small:
        load.wait()
    w1[...] = jnp.zeros_like(w1)
    w1c[...] = jnp.zeros_like(w1c)
    w2[...] = jnp.zeros_like(w2)

    def place_weights(tap, carry):
        one = first_ref[tap].T
        two = second_ref[tap].T
        for out in range(4):
            rows = pl.ds(out * 64, 192)
            lanes = pl.ds(out * 64, 64)
            w1[0, tap, rows, lanes] = one
            w2[tap, rows, lanes] = two
            if out < 2:
                w1c[tap, rows, lanes] = one
        w1[1, tap, pl.ds(0, 128), pl.ds(0, 64)] = one[:128]
        w1[1, tap, pl.ds(128, 128), pl.ds(64, 64)] = one[64:]
        w1[1, tap, pl.ds(128, 192), pl.ds(128, 64)] = one
        w1[1, tap, pl.ds(192, 192), pl.ds(192, 64)] = one
        return carry

    lax.fori_loop(0, 9, place_weights, 0)

    entry = lax.broadcasted_iota(jnp.int32, (64, 128), 0)
    lane = lax.broadcasted_iota(jnp.int32, (64, 128), 1)
    order = jnp.where(entry < 32, entry, entry - 32).astype(F32)
    angles = jnp.zeros((64, 128), F32)
    for step in range(steps):
        angles = jnp.where(lane == step, timesteps_ref[step].astype(F32), angles)
    angles = angles * jnp.exp(-math.log(10000.0) * order / 32)
    embedding = jnp.where(entry < 32, jnp.sin(angles), jnp.cos(angles))
    time_weight = time_ref[...]
    for step in range(steps):
        bias = jnp.sum(embedding[:, step : step + 1] * time_weight, axis=0, keepdims=True)
        bias_ref[step, :, pl.ds(0, 64)] = bias
        bias_ref[step, :, pl.ds(64, 64)] = bias

    row8 = lax.broadcasted_iota(jnp.int32, (8, 128), 0)
    row16 = lax.broadcasted_iota(jnp.int32, (16, 128), 0)
    lane128 = lax.broadcasted_iota(jnp.int32, (1, 128), 1)
    own_rows = pl.ds(0, 16)

    def step_body(step, carry):
        flag_x = offsets_ref[step, 0]
        flag_y = offsets_ref[step, 1]
        flag_z = offsets_ref[step, 2]
        on_x = flag_x.astype(F32)
        on_y = flag_y.astype(F32)
        on_z = flag_z.astype(F32)
        off_x = 1.0 - on_x
        cut_down = row16 == 8 * flag_y
        cut_up = row16 == 15 - 8 * flag_y
        cut_back = jnp.logical_and(row16 == 6, flag_x == 1)
        cut_ahead = jnp.logical_and(row16 == 5, flag_x == 1)
        bias = bias_ref[step]
        later = jnp.where(step + 1 < steps, timesteps_ref[jnp.minimum(step + 1, steps - 1)], 0)
        delta = jnp.full((1, 1, 128), (later - timesteps_ref[step]).astype(F32)) / 1000.0
        flat = ext.at[step].reshape(TILES, XS * YS, 128)
        flat_hidden = hidden.reshape(5, 18 * YS, 128)

        def three_rows(value):
            count = value.shape[0]
            down = pltpu.roll(value, 1, 0)[:16]
            up = pltpu.roll(value, count - 1, 0)[:16]
            return jnp.where(cut_down, 0.0, down), value[:16], jnp.where(cut_up, 0.0, up)

        def lanes_of(tile):
            return pl.ds(128 * tile, 128)

        def close_gap(taps, gap, tiles):
            lanes = pl.ds(128 * tiles[0], 128 * len(tiles))
            for tap in range(3):
                taps[tap, gap, :, lanes] = (taps[tap, gap + 2, :, lanes].astype(F32) * off_x).astype(BF16)
                taps[tap, gap + 1, :, lanes] = (taps[tap, gap - 1, :, lanes].astype(F32) * off_x).astype(BF16)

        def input_slots(tiles, keep):
            def one(x, carry):
                to = x + 2 * (x >= 8)
                for tile in tiles:
                    value = ext[step, tile, slot_of(x), own_rows]
                    if keep is not None:
                        value = value * keep
                    for tap, rows in enumerate(three_rows(value)):
                        taps_in[tap, to, :, lanes_of(tile)] = rows.astype(BF16)
                return carry

            for x in range(16):
                one(x, 0)
            close_gap(taps_in, 8, tiles)

        def inner_inputs(tiles):
            columns = []
            for tap_x in range(3):
                for tap_y in range(3):
                    for tile in tiles:
                        columns.append(jnp.concatenate([
                            taps_in[tap_y, pl.ds(tap_x, 7), :, lanes_of(tile)].reshape(112, 128),
                            taps_in[tap_y, pl.ds(9 + tap_x, 7), :, lanes_of(tile)].reshape(112, 128),
                        ], axis=0))
            return jnp.concatenate(columns, axis=1)

        def silu(total, tile):
            value = total + bias
            value = value / (1.0 + jnp.exp(-value))
            if tile == 0:
                value = value * jnp.where(lane128 < 64, on_z, 1.0)
            if tile == 4:
                value = value * jnp.where(lane128 >= 64, on_z, 1.0)
            return value

        input_slots((0, 1, 2, 3), None)
        total = jnp.dot(
            inner_inputs((0, 1)), w1[0, :, pl.ds(128, 256), :].reshape(2304, 256), preferred_element_type=F32
        )
        partial[0] = total[:, :128]
        partial[1] = total[:, 128:]
        total = jnp.dot(inner_inputs((1, 2, 3)), w1[flag_z].reshape(3456, 256), preferred_element_type=F32)
        partial[2] = total[:, :128]
        partial[3] = total[:, 128:]
        partial[4] = jnp.dot(
            inner_inputs((3,)), w1c[:, pl.ds(0, 128), :].reshape(1152, 128), preferred_element_type=F32
        )

        def outer_rows(places, tiles):
            for place in places:
                row = (22, 23, 0, 1, 14, 15, 16, 17)[place]
                for tile in tiles:
                    value = flat[tile, pl.ds(row, 16, stride=YS), :]
                    if row >= 16:
                        value = value * on_y
                    if tile >= 4:
                        value = value * on_z
                    back = jnp.where(cut_back, 0.0, pltpu.roll(value, 1, 0))
                    ahead = jnp.where(cut_ahead, 0.0, pltpu.roll(value, 15, 0))
                    for tap, rows in enumerate((back, value, ahead)):
                        edge_in[tap, place, :, lanes_of(tile)] = rows.astype(BF16)

        outer_rows((2, 3, 4, 5), range(4))

        for copy in copies(step, (0,)):
            copy.wait_recv()
        input_slots((4, 5), on_z)

        outer_rows(range(8), (4, 5))
        outer_rows((0, 1, 6, 7), range(4))

        def edge_inputs(tiles):
            columns = []
            for tap_x in range(3):
                for tap_y in range(3):
                    for tile in tiles:
                        columns.append(jnp.concatenate([
                            edge_in[tap_x, pl.ds(tap_y, 2), :, lanes_of(tile)].reshape(32, 128),
                            edge_in[tap_x, pl.ds(4 + tap_y, 2), :, lanes_of(tile)].reshape(32, 128),
                        ], axis=0))
            return jnp.concatenate(columns, axis=1)

        def keep_inner(total, tile):
            value = silu(total, tile)
            for x in range(1, 15):
                hidden[tile, slot_of(x), own_rows] = value[16 * x - 16 : 16 * x]

        def keep_edges(total, tile):
            value = silu(total, tile)
            for i, row in enumerate((23, 0, 15, 16)):
                flat_hidden[tile, pl.ds(row, 16, stride=YS), :] = value[16 * i : 16 * i + 16]

        total = jnp.dot(
            inner_inputs((5,)), w1[0, :, pl.ds(0, 128), :].reshape(1152, 256), preferred_element_type=F32
        )
        keep_inner(partial[0] + total[:, :128], 0)
        keep_inner(partial[1] + total[:, 128:], 1)
        keep_inner(partial[2], 2)
        keep_inner(partial[3], 3)
        total = jnp.dot(
            inner_inputs((4,)), w1c[:, pl.ds(128, 128), :].reshape(1152, 128), preferred_element_type=F32
        )
        keep_inner(partial[4] + total, 4)
        total = jnp.dot(edge_inputs((5, 0, 1)), w1[0].reshape(3456, 256), preferred_element_type=F32)
        keep_edges(total[:, :128], 0)
        keep_edges(total[:, 128:], 1)
        total = jnp.dot(edge_inputs((1, 2, 3)), w1[flag_z].reshape(3456, 256), preferred_element_type=F32)
        keep_edges(total[:, :128], 2)
        keep_edges(total[:, 128:], 3)
        total = jnp.dot(edge_inputs((3, 4)), w1c[...].reshape(2304, 128), preferred_element_type=F32)
        keep_edges(total, 4)

        low = jnp.where(lane128 < 64, 1.0, 1.0 - on_z)
        high = jnp.where(lane128 >= 64, 1.0, 1.0 - on_z)

        def hidden_slot(slot, to, keep_x):
            sources = ((0, None), (1, None), (2, low), (2, high), (3, None), (4, None))
            for place, (tile, keep) in enumerate(sources):
                value = hidden[tile, slot]
                if keep is not None:
                    value = value * keep
                if keep_x is not None:
                    value = value * keep_x
                for tap, rows in enumerate(three_rows(value)):
                    taps_hid[tap, to, :, lanes_of(place)] = rows.astype(BF16)

        def inner_slot(x, carry):
            hidden_slot(slot_of(x), x + 1 + 2 * (x >= 8), None)

        for x in range(1, 15):
            inner_slot(x, 0)
        close_gap(taps_hid, 9, tuple(range(6)))

        def noise_of(halves, low_slot, high_slot, slots):
            columns = []
            for tap_x in range(3):
                for tap_y in range(3):
                    columns.append(jnp.concatenate([
                        taps_hid[tap_y, pl.ds(start + tap_x, slots), :, pl.ds(384 * half, 384)].reshape(16 * slots, 384)
                        for half in halves
                        for start in (low_slot, high_slot)
                    ], axis=0))
            values = jnp.concatenate(columns, axis=1)
            return jnp.dot(values, w2[...].reshape(3456, 256), preferred_element_type=F32)

        def update(noise, half, starts, slots):
            for part in range(2):
                tile = 2 * half + part
                for i, x in enumerate(starts):
                    place = pl.ds(slot_of(x), slots)
                    change = noise[16 * slots * i : 16 * slots * (i + 1), 128 * part : 128 * part + 128]
                    before = ext[step, tile, place, own_rows]
                    ext[step + 1, tile, place, own_rows] = before + delta * change.reshape(slots, 16, 128)

        for half in range(2):
            update(noise_of((half,), 2, 10, 6), half, (2, 8), 6)

        @pl.when(step + 1 < steps)
        def _():
            for copy in copies(step + 1, (0,), INNER):
                copy.start()

        def side_slot(x, to, keep, tiles=tuple(range(TILES))):
            for tile in tiles:
                value = ext[step, tile, slot_of(x)]
                if tile >= 4:
                    value = value * on_z
                if keep is not None:
                    value = value * keep
                for tap, rows in enumerate(three_rows(value)):
                    taps_side[tap, to, :, lanes_of(tile)] = rows.astype(BF16)

        for to, x in ((2, 0), (3, 1), (4, 14), (5, 15)):
            side_slot(x, to, None)
        keep_sides = jnp.where(row8 >= 4, on_x, 1.0)

        def side_edges(tile, taps):
            scale = on_z if tile >= 4 else 1.0
            for i, tap_y in taps:
                row = (15 + tap_y) if i else (22 + tap_y) % 24
                value = flat[tile, pl.ds(12 * YS + row, 8, stride=YS), :] * (keep_sides * scale)
                first = jnp.where(row8 < 2, pltpu.roll(value, 2, 0), value)
                last = jnp.where(row8 < 2, value, pltpu.roll(value, 6, 0))
                for tap_x in range(3):
                    pair = [pltpu.roll(part, 8 - tap_x, 0) if tap_x else part for part in (first, last)]
                    rows = jnp.concatenate(pair, axis=0).astype(BF16)
                    edge_side[3 * tap_x + tap_y, pl.ds(16 * i, 16), lanes_of(tile)] = rows

        far_rows, near_rows = ((0, 0), (0, 1), (1, 1), (1, 2)), ((0, 2), (1, 0))
        halo_slots = ((0, -2), (1, -1), (6, 16), (7, 17))
        across = copies(step, (-1, 1))
        others, faces = across[:-2], across[-2:]
        for copy in others:
            copy.wait_recv()
        for to, x in halo_slots:
            side_slot(x, to, on_x, (4, 5))
        for tile in range(TILES):
            side_edges(tile, far_rows + near_rows if tile >= 4 else far_rows)

        def side_inputs(tiles):
            columns = []
            for tap_x in range(3):
                for tap_y in range(3):
                    for tile in tiles:
                        columns.append(jnp.concatenate([
                            taps_side[tap_y, pl.ds(tap_x, 2), :, lanes_of(tile)].reshape(32, 128),
                            taps_side[tap_y, pl.ds(4 + tap_x, 2), :, lanes_of(tile)].reshape(32, 128),
                            edge_side[3 * tap_x + tap_y, :, lanes_of(tile)],
                        ], axis=0))
            return jnp.concatenate(columns, axis=1)

        def keep_side(total, tile):
            value = silu(total, tile)
            for i, slot in enumerate((17, 14, 13, 16)):
                hidden[tile, slot, own_rows] = value[16 * i : 16 * i + 16]
            for i, row in enumerate((23, 16)):
                for at, slot in ((0, 17), (1, 14), (8, 13), (9, 16)):
                    place = 64 + 16 * i + at
                    hidden[tile, slot, pl.ds(row, 1)] = value[place : place + 1]

        side_partial[:, pl.ds(0, 256)] = jnp.dot(
            side_inputs((5,)), w1[0, :, pl.ds(0, 128), :].reshape(1152, 256), preferred_element_type=F32
        )
        side_partial[:, pl.ds(256, 128)] = jnp.dot(
            side_inputs((4,)), w1c[:, pl.ds(128, 128), :].reshape(1152, 128), preferred_element_type=F32
        )
        for copy in faces:
            copy.wait_recv()
        for to, x in halo_slots:
            side_slot(x, to, on_x, (0, 1, 2, 3))
        for tile in range(4):
            side_edges(tile, near_rows)
        total = side_partial[:, pl.ds(0, 256)] + jnp.dot(
            side_inputs((0, 1)), w1[0, :, pl.ds(128, 256), :].reshape(2304, 256), preferred_element_type=F32
        )
        keep_side(total[:, :128], 0)
        keep_side(total[:, 128:], 1)
        total = jnp.dot(side_inputs((1, 2, 3)), w1[flag_z].reshape(3456, 256), preferred_element_type=F32)
        keep_side(total[:, :128], 2)
        keep_side(total[:, 128:], 3)
        total = side_partial[:, pl.ds(256, 128)] + jnp.dot(
            side_inputs((3,)), w1c[:, pl.ds(0, 128), :].reshape(1152, 128), preferred_element_type=F32
        )
        keep_side(total, 4)
        hidden_slot(17, 0, on_x)
        hidden_slot(14, 1, None)
        hidden_slot(13, 18, None)
        hidden_slot(16, 19, on_x)
        noise = noise_of((0, 1), 0, 16, 2)
        for half in range(2):
            update(noise[64 * half : 64 * half + 64], half, (0, 14), 2)

            @pl.when(step + 1 < steps)
            def _():
                if half:
                    for copy in copies(step + 1, (0,), SIDES) + copies(step + 1, (-1, 1)):
                        copy.start()

        return carry

    lax.fori_loop(0, steps, step_body, 0)

    stores = [
        pltpu.make_async_copy(
            ext.at[steps, tile, pl.ds(slot_of(x), count), pl.ds(0, 16)],
            out_ref.at[pl.ds(x, count), :, pl.ds(128 * tile, 128)],
            load_sem.at[tile, i],
        )
        for tile in range(4)
        for i, (x, count) in enumerate(((2, 14), (0, 2)))
    ]
    for store in stores:
        store.start()

    def drain(step, carry):
        for copy in copies(step):
            copy.wait_send()
        return carry

    lax.fori_loop(0, steps, drain, 0)
    for store in stores:
        store.wait()


def shards(latent, conv_first, conv_second, time_weight, timesteps, offsets):
    steps = timesteps.shape[0]
    first = jnp.swapaxes(conv_first, 2, 3).reshape(9, 64, 192)
    second = jnp.swapaxes(conv_second, 2, 3).reshape(9, 64, 192)
    anywhere = pl.BlockSpec(memory_space=pl.ANY)
    count = len(DIRECTIONS)

    def body(*refs):
        kernel(steps, *refs)

    return pl.pallas_call(
        body,
        out_shape=jax.ShapeDtypeStruct(latent.shape, latent.dtype),
        in_specs=[anywhere] * 6,
        out_specs=anywhere,
        scratch_shapes=[
            pltpu.VMEM(first.shape, BF16),
            pltpu.VMEM(second.shape, BF16),
            pltpu.VMEM(time_weight.shape, F32),
            pltpu.SMEM(timesteps.shape, jnp.int32),
            pltpu.SMEM(offsets.shape, jnp.int32),
            pltpu.VMEM((steps + 1, TILES, XS, YS, 128), F32),
            pltpu.VMEM((steps, 1, 128), F32),
            pltpu.VMEM((2, 9, 384, 256), BF16),
            pltpu.VMEM((9, 256, 128), BF16),
            pltpu.VMEM((9, 384, 256), BF16),
            pltpu.VMEM((3, 18, 16, 768), BF16),
            pltpu.VMEM((3, 8, 16, 768), BF16),
            pltpu.VMEM((3, 8, 16, 768), BF16),
            pltpu.VMEM((9, 32, 768), BF16),
            pltpu.VMEM((5, 224, 128), F32),
            pltpu.VMEM((96, 384), F32),
            pltpu.VMEM((5, 18, YS, 128), F32),
            pltpu.VMEM((3, 20, 16, 768), BF16),
            pltpu.SemaphoreType.DMA((steps, count)),
            pltpu.SemaphoreType.DMA((steps, count)),
            pltpu.SemaphoreType.DMA((4, 2)),
            pltpu.SemaphoreType.DMA((5,)),
        ],
        compiler_params=pltpu.CompilerParams(
            collective_id=0, has_side_effects=True, vmem_limit_bytes=60 * 2**20
        ),
    )(latent, first, second, time_weight, timesteps, offsets)


def solution(mesh):
    return jax.shard_map(
        shards,
        mesh=mesh,
        in_specs=(P("gx", "gy", "gz"), P(), P(), P(), P(), P()),
        out_specs=P("gx", "gy", "gz"),
        check_vma=False,
    )
```

```python
import itertools
import math

import jax
import jax.numpy as jnp
from jax import lax
from jax.experimental import pallas as pl
from jax.experimental.pallas import tpu as pltpu
from jax.sharding import PartitionSpec as P

MESH = pl.DeviceIdType.MESH
F32 = jnp.float32
BF16 = jnp.bfloat16

XS, YS, TILES = 20, 24, 6


def directions():
    every = [d for d in itertools.product((-1, 0, 1), repeat=3) if d != (0, 0, 0)]
    return sorted(every, key=lambda d: (d[0] != 0, -sum(map(abs, d))))


DIRECTIONS = directions()


WHOLE, INNER, SIDES = pl.ds(0, 16), pl.ds(0, 12), pl.ds(12, 4)


def slot_of(x):
    return (x - 2) % 16 if 0 <= x < 16 else x if x >= 16 else x + 20


def sent(d, part):
    x = {-1: pl.ds(14, 2), 0: part, 1: pl.ds(12, 2)}[d[0]]
    y = {-1: pl.ds(0, 2), 0: pl.ds(0, 16), 1: pl.ds(14, 2)}[d[1]]
    z = {-1: pl.ds(0, 1), 0: pl.ds(0, 4), 1: pl.ds(3, 1)}[d[2]]
    return z, x, y


def landed(d, part):
    x = {-1: pl.ds(16, 2), 0: part, 1: pl.ds(18, 2)}[d[0]]
    y = {-1: pl.ds(16, 2), 0: pl.ds(0, 16), 1: pl.ds(22, 2)}[d[1]]
    z = {-1: pl.ds(4, 1), 0: pl.ds(0, 4), 1: pl.ds(5, 1)}[d[2]]
    return z, x, y


def surroundings():
    places = []
    for name in ("gx", "gy", "gz"):
        size, me = lax.axis_size(name), lax.axis_index(name)
        places.append((lax.rem(me + size - 1, size), me, lax.rem(me + 1, size)))
    return places


def kernel(
    steps, latent_ref, first_hbm, second_hbm, time_hbm, timesteps_hbm, offsets_hbm, out_ref,
    first_ref, second_ref, time_ref, timesteps_ref, offsets_ref, ext, bias_ref, w1, w1c, w2, taps_in, edge_in, taps_side, edge_side, partial, side_partial, hidden, taps_hid, send_sem, recv_sem, load_sem, small_sem,
):
    places = surroundings()

    def neighbour(d):
        return tuple(place[by + 1] for place, by in zip(places, d))

    barrier = pltpu.get_barrier_semaphore()
    for d in DIRECTIONS:
        pl.semaphore_signal(barrier, inc=1, device_id=neighbour(d), device_id_type=MESH)
    loads = [
        pltpu.make_async_copy(
            latent_ref.at[pl.ds(x, count), :, pl.ds(128 * tile, 128)],
            ext.at[0, tile, pl.ds(slot_of(x), count), pl.ds(0, 16)],
            load_sem.at[tile, i],
        )
        for tile in range(4)
        for i, (x, count) in enumerate(((2, 14), (0, 2)))
    ]
    small = [
        pltpu.make_async_copy(source, target, small_sem.at[i])
        for i, (source, target) in enumerate((
            (first_hbm, first_ref), (second_hbm, second_ref), (time_hbm, time_ref),
            (timesteps_hbm, timesteps_ref), (offsets_hbm, offsets_ref),
        ))
    ]
    for load in loads + small:
        load.start()
    pl.semaphore_wait(barrier, len(DIRECTIONS))
    for load in loads:
        load.wait()

    def copies(step, sides=(-1, 0, 1), part=WHOLE, heights=(-1, 0, 1)):
        return [
            pltpu.make_async_remote_copy(
                src_ref=ext.at[(step, *sent(d, part))],
                dst_ref=ext.at[(step, *landed(d, part))],
                send_sem=send_sem.at[step, i],
                recv_sem=recv_sem.at[step, i],
                device_id=neighbour(d),
                device_id_type=MESH,
            )
            for i, d in enumerate(DIRECTIONS)
            if d[0] in sides and d[2] in heights
        ]

    for copy in copies(0):
        copy.start()

    for load in small:
        load.wait()
    w1[...] = jnp.zeros_like(w1)
    w1c[...] = jnp.zeros_like(w1c)
    w2[...] = jnp.zeros_like(w2)

    def place_weights(tap, carry):
        one = first_ref[tap].T
        two = second_ref[tap].T
        for out in range(4):
            rows = pl.ds(out * 64, 192)
            lanes = pl.ds(out * 64, 64)
            w1[0, tap, rows, lanes] = one
            w2[tap, rows, lanes] = two
            if out < 2:
                w1c[tap, rows, lanes] = one
        w1[1, tap, pl.ds(0, 128), pl.ds(0, 64)] = one[:128]
        w1[1, tap, pl.ds(128, 128), pl.ds(64, 64)] = one[64:]
        w1[1, tap, pl.ds(128, 192), pl.ds(128, 64)] = one
        w1[1, tap, pl.ds(192, 192), pl.ds(192, 64)] = one
        return carry

    lax.fori_loop(0, 9, place_weights, 0)

    entry = lax.broadcasted_iota(jnp.int32, (64, 128), 0)
    lane = lax.broadcasted_iota(jnp.int32, (64, 128), 1)
    order = jnp.where(entry < 32, entry, entry - 32).astype(F32)
    angles = jnp.zeros((64, 128), F32)
    for step in range(steps):
        angles = jnp.where(lane == step, timesteps_ref[step].astype(F32), angles)
    angles = angles * jnp.exp(-math.log(10000.0) * order / 32)
    embedding = jnp.where(entry < 32, jnp.sin(angles), jnp.cos(angles))
    time_weight = time_ref[...]
    for step in range(steps):
        bias = jnp.sum(embedding[:, step : step + 1] * time_weight, axis=0, keepdims=True)
        bias_ref[step, :, pl.ds(0, 64)] = bias
        bias_ref[step, :, pl.ds(64, 64)] = bias

    row8 = lax.broadcasted_iota(jnp.int32, (8, 128), 0)
    row16 = lax.broadcasted_iota(jnp.int32, (16, 128), 0)
    lane128 = lax.broadcasted_iota(jnp.int32, (1, 128), 1)
    own_rows = pl.ds(0, 16)

    def stores(first, parts):
        return [
            pltpu.make_async_copy(
                ext.at[steps, tile, pl.ds(slot_of(x), count), pl.ds(0, 16)],
                out_ref.at[pl.ds(x, count), :, pl.ds(128 * tile, 128)],
                load_sem.at[tile, first + i],
            )
            for tile in range(4)
            for i, (x, count) in enumerate(parts)
        ]

    def step_body(step, carry):
        flag_x = offsets_ref[step, 0]
        flag_y = offsets_ref[step, 1]
        flag_z = offsets_ref[step, 2]
        on_x = flag_x.astype(F32)
        on_y = flag_y.astype(F32)
        on_z = flag_z.astype(F32)
        off_x = 1.0 - on_x
        cut_down = row16 == 8 * flag_y
        cut_up = row16 == 15 - 8 * flag_y
        cut_back = jnp.logical_and(row16 == 6, flag_x == 1)
        cut_ahead = jnp.logical_and(row16 == 5, flag_x == 1)
        bias = bias_ref[step]
        later = jnp.where(step + 1 < steps, timesteps_ref[jnp.minimum(step + 1, steps - 1)], 0)
        delta = jnp.full((1, 1, 128), (later - timesteps_ref[step]).astype(F32)) / 1000.0
        flat = ext.at[step].reshape(TILES, XS * YS, 128)
        flat_hidden = hidden.reshape(5, 18 * YS, 128)

        def three_rows(value):
            count = value.shape[0]
            down = pltpu.roll(value, 1, 0)[:16]
            up = pltpu.roll(value, count - 1, 0)[:16]
            return jnp.where(cut_down, 0.0, down), value[:16], jnp.where(cut_up, 0.0, up)

        def lanes_of(tile):
            return pl.ds(128 * tile, 128)

        def close_gap(taps, gap, tiles):
            lanes = pl.ds(128 * tiles[0], 128 * len(tiles))
            for tap in range(3):
                taps[tap, gap, :, lanes] = (taps[tap, gap + 2, :, lanes].astype(F32) * off_x).astype(BF16)
                taps[tap, gap + 1, :, lanes] = (taps[tap, gap - 1, :, lanes].astype(F32) * off_x).astype(BF16)

        def input_slots(tiles, keep):
            def one(x, carry):
                to = x + 2 * (x >= 8)
                for tile in tiles:
                    value = ext[step, tile, slot_of(x), own_rows]
                    if keep is not None:
                        value = value * keep
                    for tap, rows in enumerate(three_rows(value)):
                        taps_in[tap, to, :, lanes_of(tile)] = rows.astype(BF16)
                return carry

            for x in range(16):
                one(x, 0)
            close_gap(taps_in, 8, tiles)

        def inner_inputs(tiles):
            columns = []
            for tap_x in range(3):
                for tap_y in range(3):
                    for tile in tiles:
                        columns.append(jnp.concatenate([
                            taps_in[tap_y, pl.ds(tap_x, 7), :, lanes_of(tile)].reshape(112, 128),
                            taps_in[tap_y, pl.ds(9 + tap_x, 7), :, lanes_of(tile)].reshape(112, 128),
                        ], axis=0))
            return jnp.concatenate(columns, axis=1)

        def silu(total, tile):
            value = total + bias
            value = value / (1.0 + jnp.exp(-value))
            if tile == 0:
                value = value * jnp.where(lane128 < 64, on_z, 1.0)
            if tile == 4:
                value = value * jnp.where(lane128 >= 64, on_z, 1.0)
            return value

        input_slots((0, 1, 2, 3), None)
        total = jnp.dot(
            inner_inputs((0, 1)), w1[0, :, pl.ds(128, 256), :].reshape(2304, 256), preferred_element_type=F32
        )
        partial[0] = total[:, :128]
        partial[1] = total[:, 128:]
        total = jnp.dot(inner_inputs((1, 2, 3)), w1[flag_z].reshape(3456, 256), preferred_element_type=F32)
        partial[2] = total[:, :128]
        partial[3] = total[:, 128:]
        partial[4] = jnp.dot(
            inner_inputs((3,)), w1c[:, pl.ds(0, 128), :].reshape(1152, 128), preferred_element_type=F32
        )

        def outer_rows(places, tiles):
            for place in places:
                row = (22, 23, 0, 1, 14, 15, 16, 17)[place]
                for tile in tiles:
                    value = flat[tile, pl.ds(row, 16, stride=YS), :]
                    if row >= 16:
                        value = value * on_y
                    if tile >= 4:
                        value = value * on_z
                    back = jnp.where(cut_back, 0.0, pltpu.roll(value, 1, 0))
                    ahead = jnp.where(cut_ahead, 0.0, pltpu.roll(value, 15, 0))
                    for tap, rows in enumerate((back, value, ahead)):
                        edge_in[tap, place, :, lanes_of(tile)] = rows.astype(BF16)

        outer_rows((2, 3, 4, 5), range(4))

        for copy in copies(step, (0,)):
            copy.wait_recv()
        input_slots((4, 5), on_z)

        outer_rows(range(8), (4, 5))
        outer_rows((0, 1, 6, 7), range(4))

        def edge_inputs(tiles):
            columns = []
            for tap_x in range(3):
                for tap_y in range(3):
                    for tile in tiles:
                        columns.append(jnp.concatenate([
                            edge_in[tap_x, pl.ds(tap_y, 2), :, lanes_of(tile)].reshape(32, 128),
                            edge_in[tap_x, pl.ds(4 + tap_y, 2), :, lanes_of(tile)].reshape(32, 128),
                        ], axis=0))
            return jnp.concatenate(columns, axis=1)

        def keep_inner(total, tile):
            value = silu(total, tile)
            for x in range(1, 15):
                hidden[tile, slot_of(x), own_rows] = value[16 * x - 16 : 16 * x]

        def keep_edges(total, tile):
            value = silu(total, tile)
            for i, row in enumerate((23, 0, 15, 16)):
                flat_hidden[tile, pl.ds(row, 16, stride=YS), :] = value[16 * i : 16 * i + 16]

        total = jnp.dot(
            inner_inputs((5,)), w1[0, :, pl.ds(0, 128), :].reshape(1152, 256), preferred_element_type=F32
        )
        keep_inner(partial[0] + total[:, :128], 0)
        keep_inner(partial[1] + total[:, 128:], 1)
        keep_inner(partial[2], 2)
        keep_inner(partial[3], 3)
        total = jnp.dot(
            inner_inputs((4,)), w1c[:, pl.ds(128, 128), :].reshape(1152, 128), preferred_element_type=F32
        )
        keep_inner(partial[4] + total, 4)
        total = jnp.dot(edge_inputs((5, 0, 1)), w1[0].reshape(3456, 256), preferred_element_type=F32)
        keep_edges(total[:, :128], 0)
        keep_edges(total[:, 128:], 1)
        total = jnp.dot(edge_inputs((1, 2, 3)), w1[flag_z].reshape(3456, 256), preferred_element_type=F32)
        keep_edges(total[:, :128], 2)
        keep_edges(total[:, 128:], 3)
        total = jnp.dot(edge_inputs((3, 4)), w1c[...].reshape(2304, 128), preferred_element_type=F32)
        keep_edges(total, 4)

        low = jnp.where(lane128 < 64, 1.0, 1.0 - on_z)
        high = jnp.where(lane128 >= 64, 1.0, 1.0 - on_z)

        def hidden_slot(slot, to, keep_x):
            sources = ((0, None), (1, None), (2, low), (2, high), (3, None), (4, None))
            for place, (tile, keep) in enumerate(sources):
                value = hidden[tile, slot]
                if keep is not None:
                    value = value * keep
                if keep_x is not None:
                    value = value * keep_x
                for tap, rows in enumerate(three_rows(value)):
                    taps_hid[tap, to, :, lanes_of(place)] = rows.astype(BF16)

        def inner_slot(x, carry):
            hidden_slot(slot_of(x), x + 1 + 2 * (x >= 8), None)

        for x in range(1, 15):
            inner_slot(x, 0)
        close_gap(taps_hid, 9, tuple(range(6)))

        def noise_of(halves, starts, slots):
            columns = []
            for tap_x in range(3):
                for tap_y in range(3):
                    columns.append(jnp.concatenate([
                        taps_hid[tap_y, pl.ds(start + tap_x, slots), :, pl.ds(384 * half, 384)].reshape(16 * slots, 384)
                        for half in halves
                        for start in starts
                    ], axis=0))
            values = jnp.concatenate(columns, axis=1)
            return jnp.dot(values, w2[...].reshape(3456, 256), preferred_element_type=F32)

        def update(noise, half, starts, slots):
            for part in range(2):
                tile = 2 * half + part
                for i, x in enumerate(starts):
                    place = pl.ds(slot_of(x), slots)
                    change = noise[16 * slots * i : 16 * slots * (i + 1), 128 * part : 128 * part + 128]
                    before = ext[step, tile, place, own_rows]
                    ext[step + 1, tile, place, own_rows] = before + delta * change.reshape(slots, 16, 128)

        for start, x in ((2, 2), (10, 8)):
            noise = noise_of((0, 1), (start,), 6)
            for half in range(2):
                update(noise[96 * half : 96 * half + 96], half, (x,), 6)

        @pl.when(step + 1 < steps)
        def _():
            for copy in copies(step + 1, (0,), INNER):
                copy.start()

        @pl.when(step + 1 == steps)
        def _():
            for store in stores(2, ((2, 12),)):
                store.start()

        def side_slot(x, to, keep, tiles=tuple(range(TILES))):
            for tile in tiles:
                value = ext[step, tile, slot_of(x)]
                if tile >= 4:
                    value = value * on_z
                if keep is not None:
                    value = value * keep
                for tap, rows in enumerate(three_rows(value)):
                    taps_side[tap, to, :, lanes_of(tile)] = rows.astype(BF16)

        for to, x in ((2, 0), (3, 1), (4, 14), (5, 15)):
            side_slot(x, to, None)
        keep_sides = jnp.where(row8 >= 4, on_x, 1.0)

        def side_edges(tile, taps):
            scale = on_z if tile >= 4 else 1.0
            for i, tap_y in taps:
                row = (15 + tap_y) if i else (22 + tap_y) % 24
                value = flat[tile, pl.ds(12 * YS + row, 8, stride=YS), :] * (keep_sides * scale)
                first = jnp.where(row8 < 2, pltpu.roll(value, 2, 0), value)
                last = jnp.where(row8 < 2, value, pltpu.roll(value, 6, 0))
                for tap_x in range(3):
                    pair = [pltpu.roll(part, 8 - tap_x, 0) if tap_x else part for part in (first, last)]
                    rows = jnp.concatenate(pair, axis=0).astype(BF16)
                    edge_side[3 * tap_x + tap_y, pl.ds(16 * i, 16), lanes_of(tile)] = rows

        far_rows, near_rows = ((0, 0), (0, 1), (1, 1), (1, 2)), ((0, 2), (1, 0))
        halo_slots = ((0, -2), (1, -1), (6, 16), (7, 17))
        across = copies(step, (-1, 1))
        others, faces = across[:-2], across[-2:]
        for copy in others:
            copy.wait_recv()
        for to, x in halo_slots:
            side_slot(x, to, on_x, (4, 5))
        for tile in range(TILES):
            side_edges(tile, far_rows + near_rows if tile >= 4 else far_rows)

        def side_inputs(tiles):
            columns = []
            for tap_x in range(3):
                for tap_y in range(3):
                    for tile in tiles:
                        columns.append(jnp.concatenate([
                            taps_side[tap_y, pl.ds(tap_x, 2), :, lanes_of(tile)].reshape(32, 128),
                            taps_side[tap_y, pl.ds(4 + tap_x, 2), :, lanes_of(tile)].reshape(32, 128),
                            edge_side[3 * tap_x + tap_y, :, lanes_of(tile)],
                        ], axis=0))
            return jnp.concatenate(columns, axis=1)

        def keep_side(total, tile):
            value = silu(total, tile)
            for i, slot in enumerate((17, 14, 13, 16)):
                hidden[tile, slot, own_rows] = value[16 * i : 16 * i + 16]
            for i, row in enumerate((23, 16)):
                for at, slot in ((0, 17), (1, 14), (8, 13), (9, 16)):
                    place = 64 + 16 * i + at
                    hidden[tile, slot, pl.ds(row, 1)] = value[place : place + 1]

        side_partial[:, pl.ds(0, 256)] = jnp.dot(
            side_inputs((5,)), w1[0, :, pl.ds(0, 128), :].reshape(1152, 256), preferred_element_type=F32
        )
        side_partial[:, pl.ds(256, 128)] = jnp.dot(
            side_inputs((4,)), w1c[:, pl.ds(128, 128), :].reshape(1152, 128), preferred_element_type=F32
        )
        for copy in faces:
            copy.wait_recv()
        for to, x in halo_slots:
            side_slot(x, to, on_x, (0, 1, 2, 3))
        for tile in range(4):
            side_edges(tile, near_rows)
        total = side_partial[:, pl.ds(0, 256)] + jnp.dot(
            side_inputs((0, 1)), w1[0, :, pl.ds(128, 256), :].reshape(2304, 256), preferred_element_type=F32
        )
        keep_side(total[:, :128], 0)
        keep_side(total[:, 128:], 1)
        total = jnp.dot(side_inputs((1, 2, 3)), w1[flag_z].reshape(3456, 256), preferred_element_type=F32)
        keep_side(total[:, :128], 2)
        keep_side(total[:, 128:], 3)
        total = side_partial[:, pl.ds(256, 128)] + jnp.dot(
            side_inputs((3,)), w1c[:, pl.ds(0, 128), :].reshape(1152, 128), preferred_element_type=F32
        )
        keep_side(total, 4)
        hidden_slot(17, 0, on_x)
        hidden_slot(14, 1, None)
        hidden_slot(13, 18, None)
        hidden_slot(16, 19, on_x)
        noise = noise_of((0, 1), (0, 16), 2)
        for half in range(2):
            update(noise[64 * half : 64 * half + 64], half, (0, 14), 2)

            @pl.when(step + 1 < steps)
            def _():
                if half:
                    for copy in copies(step + 1, (0,), SIDES) + copies(step + 1, (-1, 1)):
                        copy.start()

        return carry

    lax.fori_loop(0, steps, step_body, 0)

    for store in stores(0, ((0, 2), (14, 2))):
        store.start()

    def drain(step, carry):
        for copy in copies(step):
            copy.wait_send()
        return carry

    lax.fori_loop(0, steps, drain, 0)
    for store in stores(0, ((0, 2), (14, 2))) + stores(2, ((2, 12),)):
        store.wait()


def shards(latent, conv_first, conv_second, time_weight, timesteps, offsets):
    steps = timesteps.shape[0]
    first = jnp.swapaxes(conv_first, 2, 3).reshape(9, 64, 192)
    second = jnp.swapaxes(conv_second, 2, 3).reshape(9, 64, 192)
    anywhere = pl.BlockSpec(memory_space=pl.ANY)
    count = len(DIRECTIONS)

    def body(*refs):
        kernel(steps, *refs)

    return pl.pallas_call(
        body,
        out_shape=jax.ShapeDtypeStruct(latent.shape, latent.dtype),
        in_specs=[anywhere] * 6,
        out_specs=anywhere,
        scratch_shapes=[
            pltpu.VMEM(first.shape, BF16),
            pltpu.VMEM(second.shape, BF16),
            pltpu.VMEM(time_weight.shape, F32),
            pltpu.SMEM(timesteps.shape, jnp.int32),
            pltpu.SMEM(offsets.shape, jnp.int32),
            pltpu.VMEM((steps + 1, TILES, XS, YS, 128), F32),
            pltpu.VMEM((steps, 1, 128), F32),
            pltpu.VMEM((2, 9, 384, 256), BF16),
            pltpu.VMEM((9, 256, 128), BF16),
            pltpu.VMEM((9, 384, 256), BF16),
            pltpu.VMEM((3, 18, 16, 768), BF16),
            pltpu.VMEM((3, 8, 16, 768), BF16),
            pltpu.VMEM((3, 8, 16, 768), BF16),
            pltpu.VMEM((9, 32, 768), BF16),
            pltpu.VMEM((5, 224, 128), F32),
            pltpu.VMEM((96, 384), F32),
            pltpu.VMEM((5, 18, YS, 128), F32),
            pltpu.VMEM((3, 20, 16, 768), BF16),
            pltpu.SemaphoreType.DMA((steps, count)),
            pltpu.SemaphoreType.DMA((steps, count)),
            pltpu.SemaphoreType.DMA((4, 3)),
            pltpu.SemaphoreType.DMA((5,)),
        ],
        compiler_params=pltpu.CompilerParams(
            collective_id=0, has_side_effects=True, vmem_limit_bytes=60 * 2**20
        ),
    )(latent, first, second, time_weight, timesteps, offsets)


def solution(mesh):
    return jax.shard_map(
        shards,
        mesh=mesh,
        in_specs=(P("gx", "gy", "gz"), P(), P(), P(), P(), P()),
        out_specs=P("gx", "gy", "gz"),
        check_vma=False,
    )
```

```python
import itertools
import math

import jax
import jax.numpy as jnp
from jax import lax
from jax.experimental import pallas as pl
from jax.experimental.pallas import tpu as pltpu
from jax.sharding import PartitionSpec as P

MESH = pl.DeviceIdType.MESH
F32 = jnp.float32
BF16 = jnp.bfloat16

XS, YS, TILES = 20, 24, 6


def directions():
    every = [d for d in itertools.product((-1, 0, 1), repeat=3) if d != (0, 0, 0)]
    return sorted(every, key=lambda d: (d[0] != 0, -sum(map(abs, d)), d[0] * d[1], d[0] * d[2]))


DIRECTIONS = directions()


WHOLE, INNER, SIDES = pl.ds(0, 16), pl.ds(0, 12), pl.ds(12, 4)


def slot_of(x):
    return (x - 2) % 16 if 0 <= x < 16 else x if x >= 16 else x + 20


def sent(d, part):
    x = {-1: pl.ds(14, 2), 0: part, 1: pl.ds(12, 2)}[d[0]]
    y = {-1: pl.ds(0, 2), 0: pl.ds(0, 16), 1: pl.ds(14, 2)}[d[1]]
    z = {-1: pl.ds(0, 1), 0: pl.ds(0, 4), 1: pl.ds(3, 1)}[d[2]]
    return z, x, y


def landed(d, part):
    x = {-1: pl.ds(16, 2), 0: part, 1: pl.ds(18, 2)}[d[0]]
    y = {-1: pl.ds(16, 2), 0: pl.ds(0, 16), 1: pl.ds(22, 2)}[d[1]]
    z = {-1: pl.ds(4, 1), 0: pl.ds(0, 4), 1: pl.ds(5, 1)}[d[2]]
    return z, x, y


def surroundings():
    places = []
    for name in ("gx", "gy", "gz"):
        size, me = lax.axis_size(name), lax.axis_index(name)
        places.append((lax.rem(me + size - 1, size), me, lax.rem(me + 1, size)))
    return places


def kernel(
    steps, latent_ref, first_hbm, second_hbm, time_hbm, timesteps_hbm, offsets_hbm, out_ref,
    first_ref, second_ref, time_ref, timesteps_ref, offsets_ref, ext, bias_ref, w1, w1c, w2, taps_in, edge_in, taps_side, edge_side, partial, side_partial, hidden, taps_hid, send_sem, recv_sem, load_sem, small_sem,
):
    places = surroundings()

    def neighbour(d):
        return tuple(place[by + 1] for place, by in zip(places, d))

    barrier = pltpu.get_barrier_semaphore()
    for d in DIRECTIONS:
        pl.semaphore_signal(barrier, inc=1, device_id=neighbour(d), device_id_type=MESH)
    loads = [
        pltpu.make_async_copy(
            latent_ref.at[pl.ds(x, count), :, pl.ds(128 * tile, 128)],
            ext.at[0, tile, pl.ds(slot_of(x), count), pl.ds(0, 16)],
            load_sem.at[tile, i],
        )
        for tile in range(4)
        for i, (x, count) in enumerate(((2, 14), (0, 2)))
    ]
    small = [
        pltpu.make_async_copy(source, target, small_sem.at[i])
        for i, (source, target) in enumerate((
            (first_hbm, first_ref), (second_hbm, second_ref), (time_hbm, time_ref),
            (timesteps_hbm, timesteps_ref), (offsets_hbm, offsets_ref),
        ))
    ]
    for load in loads + small:
        load.start()
    pl.semaphore_wait(barrier, len(DIRECTIONS))
    for load in loads:
        load.wait()

    def copies(step, sides=(-1, 0, 1), part=WHOLE, heights=(-1, 0, 1)):
        return [
            pltpu.make_async_remote_copy(
                src_ref=ext.at[(step, *sent(d, part))],
                dst_ref=ext.at[(step, *landed(d, part))],
                send_sem=send_sem.at[step, i],
                recv_sem=recv_sem.at[step, i],
                device_id=neighbour(d),
                device_id_type=MESH,
            )
            for i, d in enumerate(DIRECTIONS)
            if d[0] in sides and d[2] in heights
        ]

    for copy in copies(0):
        copy.start()

    for load in small:
        load.wait()
    w1[...] = jnp.zeros_like(w1)
    w1c[...] = jnp.zeros_like(w1c)
    w2[...] = jnp.zeros_like(w2)

    def place_weights(tap, carry):
        one = first_ref[tap].T
        two = second_ref[tap].T
        for out in range(4):
            rows = pl.ds(out * 64, 192)
            lanes = pl.ds(out * 64, 64)
            w1[0, tap, rows, lanes] = one
            w2[tap, rows, lanes] = two
            if out < 2:
                w1c[tap, rows, lanes] = one
        w1[1, tap, pl.ds(0, 128), pl.ds(0, 64)] = one[:128]
        w1[1, tap, pl.ds(128, 128), pl.ds(64, 64)] = one[64:]
        w1[1, tap, pl.ds(128, 192), pl.ds(128, 64)] = one
        w1[1, tap, pl.ds(192, 192), pl.ds(192, 64)] = one
        return carry

    lax.fori_loop(0, 9, place_weights, 0)

    entry = lax.broadcasted_iota(jnp.int32, (64, 128), 0)
    lane = lax.broadcasted_iota(jnp.int32, (64, 128), 1)
    order = jnp.where(entry < 32, entry, entry - 32).astype(F32)
    angles = jnp.zeros((64, 128), F32)
    for step in range(steps):
        angles = jnp.where(lane == step, timesteps_ref[step].astype(F32), angles)
    angles = angles * jnp.exp(-math.log(10000.0) * order / 32)
    embedding = jnp.where(entry < 32, jnp.sin(angles), jnp.cos(angles))
    time_weight = time_ref[...]
    for step in range(steps):
        bias = jnp.sum(embedding[:, step : step + 1] * time_weight, axis=0, keepdims=True)
        bias_ref[step, :, pl.ds(0, 64)] = bias
        bias_ref[step, :, pl.ds(64, 64)] = bias

    row8 = lax.broadcasted_iota(jnp.int32, (8, 128), 0)
    row16 = lax.broadcasted_iota(jnp.int32, (16, 128), 0)
    lane128 = lax.broadcasted_iota(jnp.int32, (1, 128), 1)
    own_rows = pl.ds(0, 16)

    def stores(first, parts):
        return [
            pltpu.make_async_copy(
                ext.at[steps, tile, pl.ds(slot_of(x), count), pl.ds(0, 16)],
                out_ref.at[pl.ds(x, count), :, pl.ds(128 * tile, 128)],
                load_sem.at[tile, first + i],
            )
            for tile in range(4)
            for i, (x, count) in enumerate(parts)
        ]

    def step_body(step, carry):
        flag_x = offsets_ref[step, 0]
        flag_y = offsets_ref[step, 1]
        flag_z = offsets_ref[step, 2]
        on_x = flag_x.astype(F32)
        on_y = flag_y.astype(F32)
        on_z = flag_z.astype(F32)
        off_x = 1.0 - on_x
        cut_down = row16 == 8 * flag_y
        cut_up = row16 == 15 - 8 * flag_y
        cut_back = jnp.logical_and(row16 == 6, flag_x == 1)
        cut_ahead = jnp.logical_and(row16 == 5, flag_x == 1)
        bias = bias_ref[step]
        later = jnp.where(step + 1 < steps, timesteps_ref[jnp.minimum(step + 1, steps - 1)], 0)
        delta = jnp.full((1, 1, 128), (later - timesteps_ref[step]).astype(F32)) / 1000.0
        flat = ext.at[step].reshape(TILES, XS * YS, 128)
        flat_hidden = hidden.reshape(5, 18 * YS, 128)

        def three_rows(value):
            count = value.shape[0]
            down = pltpu.roll(value, 1, 0)[:16]
            up = pltpu.roll(value, count - 1, 0)[:16]
            return jnp.where(cut_down, 0.0, down), value[:16], jnp.where(cut_up, 0.0, up)

        def lanes_of(tile):
            return pl.ds(128 * tile, 128)

        def close_gap(taps, gap, tiles):
            lanes = pl.ds(128 * tiles[0], 128 * len(tiles))
            for tap in range(3):
                taps[tap, gap, :, lanes] = (taps[tap, gap + 2, :, lanes].astype(F32) * off_x).astype(BF16)
                taps[tap, gap + 1, :, lanes] = (taps[tap, gap - 1, :, lanes].astype(F32) * off_x).astype(BF16)

        def input_slots(tiles, keep):
            def one(x, carry):
                to = x + 2 * (x >= 8)
                for tile in tiles:
                    value = ext[step, tile, slot_of(x), own_rows]
                    if keep is not None:
                        value = value * keep
                    for tap, rows in enumerate(three_rows(value)):
                        taps_in[tap, to, :, lanes_of(tile)] = rows.astype(BF16)
                return carry

            for x in range(16):
                one(x, 0)
            close_gap(taps_in, 8, tiles)

        def inner_inputs(tiles):
            columns = []
            for tap_x in range(3):
                for tap_y in range(3):
                    for tile in tiles:
                        columns.append(jnp.concatenate([
                            taps_in[tap_y, pl.ds(tap_x, 7), :, lanes_of(tile)].reshape(112, 128),
                            taps_in[tap_y, pl.ds(9 + tap_x, 7), :, lanes_of(tile)].reshape(112, 128),
                        ], axis=0))
            return jnp.concatenate(columns, axis=1)

        def silu(total, tile):
            value = total + bias
            value = value / (1.0 + jnp.exp(-value))
            if tile == 0:
                value = value * jnp.where(lane128 < 64, on_z, 1.0)
            if tile == 4:
                value = value * jnp.where(lane128 >= 64, on_z, 1.0)
            return value

        input_slots((0, 1, 2, 3), None)
        total = jnp.dot(
            inner_inputs((0, 1)), w1[0, :, pl.ds(128, 256), :].reshape(2304, 256), preferred_element_type=F32
        )
        partial[0] = total[:, :128]
        partial[1] = total[:, 128:]
        total = jnp.dot(inner_inputs((1, 2, 3)), w1[flag_z].reshape(3456, 256), preferred_element_type=F32)
        partial[2] = total[:, :128]
        partial[3] = total[:, 128:]
        partial[4] = jnp.dot(
            inner_inputs((3,)), w1c[:, pl.ds(0, 128), :].reshape(1152, 128), preferred_element_type=F32
        )

        def outer_rows(places, tiles):
            for place in places:
                row = (22, 23, 0, 1, 14, 15, 16, 17)[place]
                for tile in tiles:
                    value = flat[tile, pl.ds(row, 16, stride=YS), :]
                    if row >= 16:
                        value = value * on_y
                    if tile >= 4:
                        value = value * on_z
                    back = jnp.where(cut_back, 0.0, pltpu.roll(value, 1, 0))
                    ahead = jnp.where(cut_ahead, 0.0, pltpu.roll(value, 15, 0))
                    for tap, rows in enumerate((back, value, ahead)):
                        edge_in[tap, place, :, lanes_of(tile)] = rows.astype(BF16)

        outer_rows((2, 3, 4, 5), range(4))

        for copy in copies(step, (0,)):
            copy.wait_recv()
        input_slots((4, 5), on_z)

        outer_rows(range(8), (4, 5))
        outer_rows((0, 1, 6, 7), range(4))

        def edge_inputs(tiles):
            columns = []
            for tap_x in range(3):
                for tap_y in range(3):
                    for tile in tiles:
                        columns.append(jnp.concatenate([
                            edge_in[tap_x, pl.ds(tap_y, 2), :, lanes_of(tile)].reshape(32, 128),
                            edge_in[tap_x, pl.ds(4 + tap_y, 2), :, lanes_of(tile)].reshape(32, 128),
                        ], axis=0))
            return jnp.concatenate(columns, axis=1)

        def keep_inner(total, tile):
            value = silu(total, tile)
            for x in range(1, 15):
                hidden[tile, slot_of(x), own_rows] = value[16 * x - 16 : 16 * x]

        def keep_edges(total, tile):
            value = silu(total, tile)
            for i, row in enumerate((23, 0, 15, 16)):
                flat_hidden[tile, pl.ds(row, 16, stride=YS), :] = value[16 * i : 16 * i + 16]

        total = jnp.dot(
            inner_inputs((5,)), w1[0, :, pl.ds(0, 128), :].reshape(1152, 256), preferred_element_type=F32
        )
        keep_inner(partial[0] + total[:, :128], 0)
        keep_inner(partial[1] + total[:, 128:], 1)
        keep_inner(partial[2], 2)
        keep_inner(partial[3], 3)
        total = jnp.dot(
            inner_inputs((4,)), w1c[:, pl.ds(128, 128), :].reshape(1152, 128), preferred_element_type=F32
        )
        keep_inner(partial[4] + total, 4)
        total = jnp.dot(edge_inputs((5, 0, 1)), w1[0].reshape(3456, 256), preferred_element_type=F32)
        keep_edges(total[:, :128], 0)
        keep_edges(total[:, 128:], 1)
        total = jnp.dot(edge_inputs((1, 2, 3)), w1[flag_z].reshape(3456, 256), preferred_element_type=F32)
        keep_edges(total[:, :128], 2)
        keep_edges(total[:, 128:], 3)
        total = jnp.dot(edge_inputs((3, 4)), w1c[...].reshape(2304, 128), preferred_element_type=F32)
        keep_edges(total, 4)

        low = jnp.where(lane128 < 64, 1.0, 1.0 - on_z)
        high = jnp.where(lane128 >= 64, 1.0, 1.0 - on_z)

        def hidden_slot(slot, to, keep_x):
            sources = ((0, None), (1, None), (2, low), (2, high), (3, None), (4, None))
            for place, (tile, keep) in enumerate(sources):
                value = hidden[tile, slot]
                if keep is not None:
                    value = value * keep
                if keep_x is not None:
                    value = value * keep_x
                for tap, rows in enumerate(three_rows(value)):
                    taps_hid[tap, to, :, lanes_of(place)] = rows.astype(BF16)

        def inner_slot(x, carry):
            hidden_slot(slot_of(x), x + 1 + 2 * (x >= 8), None)

        for x in range(1, 15):
            inner_slot(x, 0)
        close_gap(taps_hid, 9, tuple(range(6)))

        def noise_of(halves, starts, slots):
            columns = []
            for tap_x in range(3):
                for tap_y in range(3):
                    columns.append(jnp.concatenate([
                        taps_hid[tap_y, pl.ds(start + tap_x, slots), :, pl.ds(384 * half, 384)].reshape(16 * slots, 384)
                        for half in halves
                        for start in starts
                    ], axis=0))
            values = jnp.concatenate(columns, axis=1)
            return jnp.dot(values, w2[...].reshape(3456, 256), preferred_element_type=F32)

        def update(noise, half, starts, slots):
            for part in range(2):
                tile = 2 * half + part
                for i, x in enumerate(starts):
                    place = pl.ds(slot_of(x), slots)
                    change = noise[16 * slots * i : 16 * slots * (i + 1), 128 * part : 128 * part + 128]
                    before = ext[step, tile, place, own_rows]
                    ext[step + 1, tile, place, own_rows] = before + delta * change.reshape(slots, 16, 128)

        for start, x in ((2, 2), (10, 8)):
            noise = noise_of((0, 1), (start,), 6)
            for half in range(2):
                update(noise[96 * half : 96 * half + 96], half, (x,), 6)

        @pl.when(step + 1 < steps)
        def _():
            for copy in copies(step + 1, (0,), INNER):
                copy.start()

        @pl.when(step + 1 == steps)
        def _():
            for store in stores(2, ((2, 12),)):
                store.start()

        def side_slot(x, to, keep, tiles=tuple(range(TILES))):
            for tile in tiles:
                value = ext[step, tile, slot_of(x)]
                if tile >= 4:
                    value = value * on_z
                if keep is not None:
                    value = value * keep
                for tap, rows in enumerate(three_rows(value)):
                    taps_side[tap, to, :, lanes_of(tile)] = rows.astype(BF16)

        for to, x in ((2, 0), (3, 1), (4, 14), (5, 15)):
            side_slot(x, to, None)
        keep_sides = jnp.where(row8 >= 4, on_x, 1.0)

        def side_edges(tile, taps):
            scale = on_z if tile >= 4 else 1.0
            for i, tap_y in taps:
                row = (15 + tap_y) if i else (22 + tap_y) % 24
                value = flat[tile, pl.ds(12 * YS + row, 8, stride=YS), :] * (keep_sides * scale)
                first = jnp.where(row8 < 2, pltpu.roll(value, 2, 0), value)
                last = jnp.where(row8 < 2, value, pltpu.roll(value, 6, 0))
                for tap_x in range(3):
                    pair = [pltpu.roll(part, 8 - tap_x, 0) if tap_x else part for part in (first, last)]
                    rows = jnp.concatenate(pair, axis=0).astype(BF16)
                    edge_side[3 * tap_x + tap_y, pl.ds(16 * i, 16), lanes_of(tile)] = rows

        far_rows, near_rows = ((0, 0), (0, 1), (1, 1), (1, 2)), ((0, 2), (1, 0))
        halo_slots = ((0, -2), (1, -1), (6, 16), (7, 17))
        across = copies(step, (-1, 1))
        others, faces = across[:-2], across[-2:]
        for copy in others:
            copy.wait_recv()
        for to, x in halo_slots:
            side_slot(x, to, on_x, (4, 5))
        for tile in range(TILES):
            side_edges(tile, far_rows + near_rows if tile >= 4 else far_rows)

        def side_inputs(tiles):
            columns = []
            for tap_x in range(3):
                for tap_y in range(3):
                    for tile in tiles:
                        columns.append(jnp.concatenate([
                            taps_side[tap_y, pl.ds(tap_x, 2), :, lanes_of(tile)].reshape(32, 128),
                            taps_side[tap_y, pl.ds(4 + tap_x, 2), :, lanes_of(tile)].reshape(32, 128),
                            edge_side[3 * tap_x + tap_y, :, lanes_of(tile)],
                        ], axis=0))
            return jnp.concatenate(columns, axis=1)

        def keep_side(total, tile):
            value = silu(total, tile)
            for i, slot in enumerate((17, 14, 13, 16)):
                hidden[tile, slot, own_rows] = value[16 * i : 16 * i + 16]
            for i, row in enumerate((23, 16)):
                for at, slot in ((0, 17), (1, 14), (8, 13), (9, 16)):
                    place = 64 + 16 * i + at
                    hidden[tile, slot, pl.ds(row, 1)] = value[place : place + 1]

        side_partial[:, pl.ds(0, 256)] = jnp.dot(
            side_inputs((5,)), w1[0, :, pl.ds(0, 128), :].reshape(1152, 256), preferred_element_type=F32
        )
        side_partial[:, pl.ds(256, 128)] = jnp.dot(
            side_inputs((4,)), w1c[:, pl.ds(128, 128), :].reshape(1152, 128), preferred_element_type=F32
        )
        for copy in faces:
            copy.wait_recv()
        for to, x in halo_slots:
            side_slot(x, to, on_x, (0, 1, 2, 3))
        for tile in range(4):
            side_edges(tile, near_rows)
        total = side_partial[:, pl.ds(0, 256)] + jnp.dot(
            side_inputs((0, 1)), w1[0, :, pl.ds(128, 256), :].reshape(2304, 256), preferred_element_type=F32
        )
        keep_side(total[:, :128], 0)
        keep_side(total[:, 128:], 1)
        total = jnp.dot(side_inputs((1, 2, 3)), w1[flag_z].reshape(3456, 256), preferred_element_type=F32)
        keep_side(total[:, :128], 2)
        keep_side(total[:, 128:], 3)
        total = side_partial[:, pl.ds(256, 128)] + jnp.dot(
            side_inputs((3,)), w1c[:, pl.ds(0, 128), :].reshape(1152, 128), preferred_element_type=F32
        )
        keep_side(total, 4)
        hidden_slot(17, 0, on_x)
        hidden_slot(14, 1, None)
        hidden_slot(13, 18, None)
        hidden_slot(16, 19, on_x)
        noise = noise_of((0, 1), (0, 16), 2)
        for half in range(2):
            update(noise[64 * half : 64 * half + 64], half, (0, 14), 2)

            @pl.when(step + 1 < steps)
            def _():
                if half:
                    for copy in copies(step + 1, (0,), SIDES) + copies(step + 1, (-1, 1)):
                        copy.start()

        return carry

    lax.fori_loop(0, steps, step_body, 0)

    for store in stores(0, ((0, 2), (14, 2))):
        store.start()

    def drain(step, carry):
        for copy in copies(step):
            copy.wait_send()
        return carry

    lax.fori_loop(0, steps, drain, 0)
    for store in stores(0, ((0, 2), (14, 2))) + stores(2, ((2, 12),)):
        store.wait()


def shards(latent, conv_first, conv_second, time_weight, timesteps, offsets):
    steps = timesteps.shape[0]
    first = jnp.swapaxes(conv_first, 2, 3).reshape(9, 64, 192)
    second = jnp.swapaxes(conv_second, 2, 3).reshape(9, 64, 192)
    anywhere = pl.BlockSpec(memory_space=pl.ANY)
    count = len(DIRECTIONS)

    def body(*refs):
        kernel(steps, *refs)

    return pl.pallas_call(
        body,
        out_shape=jax.ShapeDtypeStruct(latent.shape, latent.dtype),
        in_specs=[anywhere] * 6,
        out_specs=anywhere,
        scratch_shapes=[
            pltpu.VMEM(first.shape, BF16),
            pltpu.VMEM(second.shape, BF16),
            pltpu.VMEM(time_weight.shape, F32),
            pltpu.SMEM(timesteps.shape, jnp.int32),
            pltpu.SMEM(offsets.shape, jnp.int32),
            pltpu.VMEM((steps + 1, TILES, XS, YS, 128), F32),
            pltpu.VMEM((steps, 1, 128), F32),
            pltpu.VMEM((2, 9, 384, 256), BF16),
            pltpu.VMEM((9, 256, 128), BF16),
            pltpu.VMEM((9, 384, 256), BF16),
            pltpu.VMEM((3, 18, 16, 768), BF16),
            pltpu.VMEM((3, 8, 16, 768), BF16),
            pltpu.VMEM((3, 8, 16, 768), BF16),
            pltpu.VMEM((9, 32, 768), BF16),
            pltpu.VMEM((5, 224, 128), F32),
            pltpu.VMEM((96, 384), F32),
            pltpu.VMEM((5, 18, YS, 128), F32),
            pltpu.VMEM((3, 20, 16, 768), BF16),
            pltpu.SemaphoreType.DMA((steps, count)),
            pltpu.SemaphoreType.DMA((steps, count)),
            pltpu.SemaphoreType.DMA((4, 3)),
            pltpu.SemaphoreType.DMA((5,)),
        ],
        compiler_params=pltpu.CompilerParams(
            collective_id=0, has_side_effects=True, vmem_limit_bytes=60 * 2**20
        ),
    )(latent, first, second, time_weight, timesteps, offsets)


def solution(mesh):
    return jax.shard_map(
        shards,
        mesh=mesh,
        in_specs=(P("gx", "gy", "gz"), P(), P(), P(), P(), P()),
        out_specs=P("gx", "gy", "gz"),
        check_vma=False,
    )
```
